128 devices in a mesh: batch: 2 (over core), ctx: 64 (over x, y, z).
Axes of the slice: x: 4, y: 4, z: 4, core: 2. Of those that a mesh axis runs over, the one named last changes fastest.
Arguments:
- tokens: int32 [4, 16384], P('batch', 'ctx'), parts along dimension 0, may hold values from 65 to 116, as said below
- lengths: int32 [4], P('batch'), parts along dimension 0, may hold values from 4096 to 16384, as said below
- feature_table: bfloat16 [512, 12288], replicated, may hold values from -6 to 6
- short_filter: float32 [3, 12288], replicated, may hold values from -3 to 3
- long_filter: bfloat16 [256, 128], replicated, may hold values from -0.5 to 0.5
- queries: bfloat16 [64, 4096], replicated, may hold values from -210 to 210
Outputs:
- mixer_field: bfloat16 [4, 16384, 4096], P('batch', 'ctx'), parts along dimension 0
- pooled: float32 [4, 64, 4096], P('batch'), parts along dimension 0
The draws below stay inside these ranges and needn't reach their ends.
There are 2 independent parts, one for each index of `batch`. The reference program is written for one: setup_inputs(seed, part) draws one part's arguments, and reference() takes and returns one part's arrays. A program takes and returns all parts, laid end to end along the dimension named above; an argument that names none is the same for every part. Nothing has to cross between parts.
Inputs may be any that keep to these rules, and one draw needn't show every extreme that they name: `tokens`: every token is the byte code of one of the bases A, C, G, T in upper or lower case. `lengths`: in every part at least one window has all 16384 positions valid.
All inputs are finite; a program needn't handle non-finite values.
Results may differ from the reference program's by a relative error of at most 0.0065.
The reference program's roundings to bfloat16 on the way (of `features`, `gated` and `weights`) count: a program that leaves them out, or rounds other values in their place, can miss the bound.
Values may be sent and summed in bfloat16 or wider, within the bound.
A program may use at most 192 MiB of HBM per device.

```python
import jax
import jax.numpy as jnp
from jax import lax

D = 4096
VOCAB = 512
GROUPS = 256
TAPS = 128
NQ = 64
WIN = 2
LENGTH = 16384


def draw_tokens(key, part):
    choice_index = jax.random.randint(key, (WIN, LENGTH), 0, 8)
    codes = jnp.array([65, 67, 71, 84, 97, 99, 103, 116], jnp.int32)
    return codes[choice_index]


def draw_lengths(key, part):
    first_key, second_key = jax.random.split(jax.random.fold_in(key, 11))
    drawn = jax.random.randint(first_key, (WIN,), LENGTH // 4, LENGTH + 1)
    full_window = jax.random.randint(second_key, (), 0, WIN)
    return jnp.where(jnp.arange(WIN) == full_window, LENGTH, drawn).astype(jnp.int32)


def draw_queries(key, part):
    base_key = jax.random.fold_in(jax.random.fold_in(key, 23), 0)
    base = jnp.clip(jax.random.normal(base_key, (NQ, D), jnp.float32), -6.0, 6.0)
    return (base * 4.0).astype(jnp.bfloat16)


def normal_values(stream_key, shape, spread, reach, held_as=jnp.bfloat16):
    values = jax.random.normal(stream_key, shape, jnp.float32) * spread
    return jnp.minimum(jnp.maximum(values, -reach), reach).astype(held_as)


def setup_inputs(seed: int = 0, part: int = 0) -> dict:
    keys = jax.random.split(jax.random.key(seed), 7)
    part_keys = jax.random.split(jax.random.fold_in(keys[6], part), 7)
    tokens = draw_tokens(jax.random.fold_in(jax.random.fold_in(keys[6], part), 71), part)
    lengths = draw_lengths(jax.random.fold_in(jax.random.fold_in(keys[6], part), 71), part)
    feature_table = normal_values(keys[2], (VOCAB, 3 * D), 1.0, 6.0)
    short_filter = normal_values(keys[3], (3, 3 * D), 0.6, 3.0, jnp.float32)
    long_filter = normal_values(keys[4], (GROUPS, TAPS), TAPS ** -0.5, 0.5)
    queries = draw_queries(jax.random.fold_in(keys[6], 71), part)
    return dict(tokens=tokens, lengths=lengths, feature_table=feature_table, short_filter=short_filter, long_filter=long_filter, queries=queries)


def kernel_rows(long_filter):
    tap_count = long_filter.shape[1]
    out_pos = jnp.arange(tap_count)[:, None]
    in_pos = jnp.arange(2 * tap_count)[None, :]
    offset = out_pos + tap_count - in_pos
    usable = (offset >= 0) & (offset < tap_count)
    picked = jnp.take(long_filter, jnp.clip(offset, 0, tap_count - 1).astype(jnp.int32), axis=1)
    return jnp.where(usable[None], picked, jnp.zeros_like(picked))

def reference(tokens, lengths, feature_table, short_filter, long_filter, queries):
    model_width = feature_table.shape[1] // 3
    tap_count = long_filter.shape[1]
    group_count = long_filter.shape[0]
    group_width = model_width // group_count
    kernel = kernel_rows(long_filter).astype(jnp.float32)

    def one_window(pair):
        window_tokens, window_length = pair
        total = window_tokens.shape[0]
        features = jnp.take(feature_table, window_tokens, axis=0)
        padded = jnp.concatenate([jnp.zeros((2, 3 * model_width), features.dtype), features], axis=0)
        featurized = short_filter[0] * padded[2:] + short_filter[1] * padded[1:total + 1] + short_filter[2] * padded[:total]
        gated = (featurized[:, model_width:2 * model_width] * featurized[:, 2 * model_width:]).astype(jnp.bfloat16)
        extended = jnp.concatenate([jnp.zeros((tap_count, model_width), jnp.bfloat16), gated], axis=0).astype(jnp.float32)
        block_count = total // tap_count
        previous = extended[:total].reshape(block_count, tap_count, group_count, group_width)
        current = extended[tap_count:].reshape(block_count, tap_count, group_count, group_width)
        convolved = jnp.einsum('gim,bmgc->bigc', kernel[:, :, :tap_count], previous, precision=lax.Precision.HIGHEST)
        convolved = convolved + jnp.einsum('gim,bmgc->bigc', kernel[:, :, tap_count:], current, precision=lax.Precision.HIGHEST)
        convolved = convolved.reshape(total, model_width)
        mixer_field = (featurized[:, :model_width] * convolved).astype(jnp.bfloat16)
        scores = jnp.dot(queries, mixer_field.T, preferred_element_type=jnp.float32) * model_width ** (-0.5)
        is_valid = (jnp.arange(total) < window_length)[None, :]
        row_top = lax.optimization_barrier(jnp.max(jnp.where(is_valid, scores, -jnp.inf), axis=1))
        shifted = jnp.where(is_valid, scores - row_top[:, None], 0.0)
        weights = jnp.where(is_valid, jnp.exp(shifted), 0.0).astype(jnp.bfloat16)
        weighted = jnp.dot(weights, mixer_field, preferred_element_type=jnp.float32)
        pooled = weighted / jnp.sqrt(lax.optimization_barrier(jnp.mean(weighted * weighted, axis=1, keepdims=True)) + 1e-06)
        return (mixer_field, pooled)
    mixer_field, pooled = lax.map(one_window, (tokens, lengths))
    return (mixer_field, pooled)
```

```python
import functools

import jax
import jax.numpy as jnp
from jax import lax
from jax.experimental import pallas as pl
from jax.experimental.pallas import tpu as pltpu
from jax.sharding import PartitionSpec as P

bf16, f32 = jnp.bfloat16, jnp.float32
CODES = (65, 67, 71, 84, 97, 99, 103, 116)
STRIDES = (16, 4, 1)
MESH = pl.DeviceIdType.MESH
CB = 256
GPC = CB // 16
T = 128
LOWEST = -1e38


def prep_kernel(tok_ref, table_ref, sf_ref, oh_ref, tab_ref, rows_s, prev_s, load_sem, send_sem, recv_sem):
    me = lax.axis_index("ctx")
    core = lax.axis_index("batch")
    nxt, prv = lax.rem(me + 1, 64), lax.rem(me + 63, 64)
    load = pltpu.make_async_copy(table_ref.at[pl.ds(64, 64)], rows_s, load_sem)
    load.start()
    barrier = pltpu.get_barrier_semaphore()
    pl.semaphore_signal(barrier, inc=1, device_id=(core, prv), device_id_type=MESH)
    pl.semaphore_wait(barrier, 1)
    send = pltpu.make_async_remote_copy(
        src_ref=tok_ref, dst_ref=prev_s, send_sem=send_sem, recv_sem=recv_sem,
        device_id=(core, nxt), device_id_type=MESH)
    send.start()
    load.wait()
    sel_row = lax.broadcasted_iota(jnp.int32, (32, 64), 0)
    sel_col = lax.broadcasted_iota(jnp.int32, (32, 64), 1)
    want = jnp.full((32, 64), -1, jnp.int32)
    for n in range(24):
        want = jnp.where(sel_row == n, CODES[n % 8] - 64, want)
    select = jnp.where(sel_col == want, 1.0, 0.0).astype(bf16)
    e_r = lax.broadcasted_iota(jnp.int32, (T, T), 0)
    e_c = lax.broadcasted_iota(jnp.int32, (T, T), 1)
    eye = jnp.where(e_r == e_c, 1.0, 0.0).astype(bf16)

    @pl.loop(0, 48)
    def _(step):
        for u in range(2):
            cols = pl.ds(pl.multiple_of((2 * step + u) * T, T), T)
            picked = jnp.dot(select, rows_s[:, cols], preferred_element_type=f32)[:24]
            gains = jnp.concatenate([jnp.broadcast_to(sf_ref[n:n + 1, cols], (8, T)) for n in range(3)], axis=0)
            prod = picked * gains
            hi = prod.astype(bf16).astype(f32)
            rest = prod - hi
            mid = rest.astype(bf16).astype(f32)
            low = rest - mid
            stacked = jnp.concatenate([hi, mid, low, jnp.zeros((56, T), f32)], axis=0).astype(bf16)
            turned = lax.dot_general(eye, stacked, (((1,), (1,)), ((), ())), preferred_element_type=f32)
            tab_ref[cols, :] = turned.astype(bf16)

    send.wait()
    codes = jnp.zeros((8, 384), jnp.int32)
    code_row = lax.broadcasted_iota(jnp.int32, (8, 384), 0)
    for n in range(8):
        codes = jnp.where(code_row == n, CODES[n], codes)
    prev = jnp.where(me == 0, -1, prev_s[...])
    for w in range(2):
        ext = jnp.concatenate([prev[w:w + 1], tok_ref[w:w + 1]], axis=1)
        hot = [jnp.where(jnp.broadcast_to(ext[:, 128 - k:512 - k], (8, 384)) == codes, 1.0, 0.0) for k in range(3)]
        full = jnp.concatenate(hot * 3 + [jnp.zeros((8, 384), f32)], axis=0).astype(bf16)
        oh_ref[:, 128 * w:128 * w + 128] = full[:, :128]
        oh_ref[:, 256 + 256 * w:512 + 256 * w] = full[:, 128:]


def prep_call(tokens, table, short_filter):
    vmem = pl.BlockSpec(memory_space=pltpu.VMEM)
    return pl.pallas_call(
        prep_kernel,
        in_specs=[vmem, pl.BlockSpec(memory_space=pl.ANY), vmem],
        out_specs=[vmem, vmem],
        out_shape=[jax.ShapeDtypeStruct((80, 768), bf16), jax.ShapeDtypeStruct((12288, 128), bf16)],
        scratch_shapes=[pltpu.VMEM((64, 12288), bf16), pltpu.VMEM((2, 256), jnp.int32),
                        pltpu.SemaphoreType.DMA, pltpu.SemaphoreType.DMA, pltpu.SemaphoreType.DMA],
        compiler_params=pltpu.CompilerParams(collective_id=0, has_side_effects=True, vmem_limit_bytes=32 * 2**20),
    )(tokens, table, short_filter)


def main_kernel(first_ref, len_ref, oh_ref, tq_ref, tk_ref, tv_ref, h_ref, qry_ref,
                mix_ref, part_ref, m_s, s_s, g_s):
    i = pl.program_id(0)
    steps = pl.num_programs(0)
    oh = oh_ref[...]
    dot = functools.partial(jnp.dot, preferred_element_type=f32)
    k = dot(tk_ref[...][:, :80], oh)
    v = dot(tv_ref[...][:, :80], oh)
    g_s[...] = (k * v).astype(bf16)
    s_i = lax.broadcasted_iota(jnp.int32, (T, T), 0)
    t_i = lax.broadcasted_iota(jnp.int32, (T, T), 1)
    upper = t_i >= s_i
    h = h_ref[...].astype(f32)
    base = i * CB
    for j in range(GPC):
        circ = pltpu.roll(jnp.broadcast_to(h[j:j + 1], (T, T)), 0, 1, stride=1, stride_axis=0)
        toep = jnp.concatenate([jnp.where(upper, 0.0, circ), jnp.where(upper, circ, 0.0)], axis=0).astype(bf16)
        rows = pl.ds(16 * j, 16)
        q = dot(tq_ref[rows, :][:, :80], oh[:, 256:])
        blk = [g_s[rows, pl.ds(T * b, T)] for b in range(6)]
        lhs = jnp.concatenate([
            jnp.concatenate([blk[0], blk[2]], axis=1),
            jnp.concatenate([blk[2], blk[3]], axis=1),
            jnp.concatenate([blk[1], blk[4]], axis=1),
            jnp.concatenate([blk[4], blk[5]], axis=1)], axis=0)
        conv = dot(lhs, toep)
        conv = jnp.concatenate([conv[16 * b:16 * b + 16] for b in range(4)], axis=1)
        m_s[pl.ds(pl.multiple_of(base + 16 * j, 16), 16), :] = (q * conv).astype(bf16)
    m = m_s[pl.ds(pl.multiple_of(base, CB), CB), :]
    sc = dot(qry_ref[...], m)

    @pl.when(i == 0)
    def _():
        s_s[...] = sc

    @pl.when(i > 0)
    def _():
        s_s[...] += sc
    for w in range(2):
        mix_ref[w] = m[:, 256 * w:256 * w + 256].T

    @pl.when(i == steps - 1)
    def _():
        pos = lax.broadcasted_iota(jnp.int32, (64, 256), 1) + first_ref[0]
        for w in range(2):
            s = s_s[:, 256 * w:256 * w + 256] * (4096 ** -0.5)
            ok = pos < len_ref[w]
            top = jnp.max(jnp.where(ok, s, LOWEST), axis=1, keepdims=True)
            shifted = jnp.where(ok, s - top, 0.0)
            wt = jnp.where(ok, jnp.exp(shifted), 0.0).astype(bf16)
            for hb in range(2):
                for c in range(8):
                    cs = hb * 2048 + c * 256
                    r = lax.dot_general(wt, m_s[cs:cs + 256, 256 * w:256 * w + 256], (((1,), (1,)), ((), ())), preferred_element_type=f32).astype(bf16)
                    for p in range(4):
                        for u in range(2):
                            part_ref[2 * w + hb, p, 2 * c + u] = r[16 * p:16 * p + 16, 128 * u:128 * u + 128]
            hi = top.astype(bf16).astype(f32)
            mid = (top - hi).astype(bf16).astype(f32)
            lo = (top - hi - mid)
            lane = lax.broadcasted_iota(jnp.int32, (64, 128), 1)
            tile = jnp.where(lane == 0, hi, jnp.where(lane == 1, mid, jnp.where(lane == 2, lo, 0.0))).astype(bf16)
            for hb in range(2):
                for p in range(4):
                    part_ref[2 * w + hb, p, 16] = tile[16 * p:16 * p + 16]

def main_call(first, lengths, oh, tab, h, qry):
    n = 4096 // CB
    smem = pl.BlockSpec(memory_space=pltpu.SMEM)
    return pl.pallas_call(
        main_kernel, grid=(n,),
        in_specs=[smem, smem,
            pl.BlockSpec((80, 768), lambda i: (0, 0)),
            pl.BlockSpec((CB, 128), lambda i: (i, 0)),
            pl.BlockSpec((CB, 128), lambda i: (i + n, 0)),
            pl.BlockSpec((CB, 128), lambda i: (i + 2 * n, 0)),
            pl.BlockSpec((GPC, 128), lambda i: (i, 0)),
            pl.BlockSpec((64, CB), lambda i: (0, i))],
        out_specs=[pl.BlockSpec((2, 256, CB), lambda i: (0, 0, i)),
                   pl.BlockSpec((4, 4, 17, 16, 128), lambda i: (0, 0, 0, 0, 0))],
        out_shape=[jax.ShapeDtypeStruct((2, 256, 4096), bf16), jax.ShapeDtypeStruct((4, 4, 17, 16, 128), bf16)],
        scratch_shapes=[pltpu.VMEM((4096, 512), bf16), pltpu.VMEM((64, 512), f32), pltpu.VMEM((CB, 768), bf16)],
        compiler_params=pltpu.CompilerParams(vmem_limit_bytes=48 * 2**20, dimension_semantics=("arbitrary",)),
    )(first, lengths, oh, tab, tab, tab, h, qry)


def exchange_kernel(part_ref, out_ref, own_s, r1, s1f, s2, r2, s2f, s3, r3, own_sem, send_sem, recv_sem):
    me = lax.axis_index("ctx")
    core = lax.axis_index("batch")
    coord = [lax.rem(me // st, 4) for st in STRIDES]
    peer = [[me + (lax.rem(coord[a] + d, 4) - coord[a]) * STRIDES[a] for d in range(4)] for a in range(3)]

    def mixed(values, p, stage):
        first, second = values[(p + stage) % 3], values[(p + stage + 1) % 3]
        return first + core * (second - first)

    mine = [[mixed(coord, p, s) for s in range(3)] for p in range(4)]
    peers = [[[mixed([peer[a][d] for a in range(3)], p, s) for d in range(4)] for s in range(3)] for p in range(4)]
    barrier = pltpu.get_barrier_semaphore()
    for a in range(3):
        for d in range(1, 4):
            pl.semaphore_signal(barrier, inc=1, device_id=(core, peer[a][d]), device_id_type=MESH)
    pl.semaphore_wait(barrier, 9)
    sends = []

    def remote(src, dst, phase, p, d, stage):
        return pltpu.make_async_remote_copy(
            src_ref=src, dst_ref=dst, send_sem=send_sem.at[phase, p, d - 1], recv_sem=recv_sem.at[phase, p, d - 1],
            device_id=(core, peers[p][stage][d]), device_id_type=MESH)

    def go(*args):
        copy = remote(*args)
        copy.start()
        sends.append(copy)

    own = []
    for p in range(4):
        for d in (2, 1, 3):
            go(part_ref.at[lax.rem(mine[p][0] + d, 4), p], r1.at[p, d - 1], 0, p, d, 0)
    for p in range(4):
        copy = pltpu.make_async_copy(part_ref.at[mine[p][0], p], own_s.at[p], own_sem.at[p])
        copy.start()
        own.append(copy)
    lane = lax.broadcasted_iota(jnp.int32, (16, 128), 1)

    def top_tile(top):
        hi = top.astype(bf16).astype(f32)
        mid = (top - hi).astype(bf16).astype(f32)
        low = top - hi - mid
        return jnp.where(lane == 0, hi, jnp.where(lane == 1, mid, jnp.where(lane == 2, low, 0.0))).astype(bf16)

    def read_top(tile):
        return jnp.sum(tile.astype(f32), axis=1, keepdims=True)

    def merged(tops):
        top = functools.reduce(jnp.maximum, tops)
        return top, [jnp.exp(t - top) for t in tops]

    tops1 = []
    for p in range(4):
        own[p].wait()
        for d in (1, 2, 3):
            remote(own_s.at[p], r1.at[p, d - 1], 0, p, d, 0).wait_recv()
        sources = [own_s.at[p]] + [r1.at[p, d] for d in range(3)]
        top, gains = merged([read_top(s[16]) for s in sources])
        tops1.append(top)
        tile = top_tile(top)
        for j in range(4):
            for i in range(4):
                total = sum(g * s[4 * j + i].astype(f32) for g, s in zip(gains, sources))
                s1f[p, j, i] = total
                s2[p, j, i] = total.astype(bf16)
            s2[p, j, 4] = tile
        for d in (2, 1, 3):
            go(s2.at[p, lax.rem(mine[p][1] + d, 4)], r2.at[p, d - 1], 1, p, d, 1)
    tops2 = []
    for p in range(4):
        for d in (1, 2, 3):
            remote(s2.at[p, 0], r2.at[p, d - 1], 1, p, d, 1).wait_recv()
        top, gains = merged([tops1[p]] + [read_top(r2[p, d, 4]) for d in range(3)])
        tops2.append(top)
        tile = top_tile(top)
        for i in range(4):
            total = gains[0] * s1f[p, mine[p][1], i]
            for d in range(3):
                total += gains[d + 1] * r2[p, d, i].astype(f32)
            s2f[p, i] = total
            s3[p, i, 0] = total.astype(bf16)
            s3[p, i, 1] = tile
        for d in (2, 1, 3):
            go(s3.at[p, lax.rem(mine[p][2] + d, 4)], r3.at[p, d - 1], 2, p, d, 2)
    for p in range(4):
        for d in (1, 2, 3):
            remote(s3.at[p, 0], r3.at[p, d - 1], 2, p, d, 2).wait_recv()
        top, gains = merged([tops2[p]] + [read_top(r3[p, d, 1]) for d in range(3)])
        total = gains[0] * s2f[p, mine[p][2]]
        for d in range(3):
            total += gains[d + 1] * r3[p, d, 0].astype(f32)
        spot = out_ref.at[p, mine[p][0], mine[p][1], mine[p][2]]
        spot[...] = total.astype(bf16)
        for d in (2, 1, 3):
            go(spot, spot, 3, p, d, 2)
    for p in range(4):
        for d in (1, 2, 3):
            spot = out_ref.at[p, mine[p][0], mine[p][1], lax.rem(mine[p][2] + 4 - d, 4)]
            remote(spot, spot, 3, p, d, 2).wait_recv()
        spot = out_ref.at[p, mine[p][0], mine[p][1]]
        for d in (2, 1, 3):
            go(spot, spot, 4, p, d, 1)
    for p in range(4):
        for d in (1, 2, 3):
            spot = out_ref.at[p, mine[p][0], lax.rem(mine[p][1] + 4 - d, 4)]
            remote(spot, spot, 4, p, d, 1).wait_recv()
        spot = out_ref.at[p, mine[p][0]]
        for d in (2, 1, 3):
            go(spot, spot, 5, p, d, 0)
    for p in range(4):
        for d in (1, 2, 3):
            spot = out_ref.at[p, lax.rem(mine[p][0] + 4 - d, 4)]
            remote(spot, spot, 5, p, d, 0).wait_recv()
    for copy in sends:
        copy.wait_send()


def exchange_call(part):
    return pl.pallas_call(
        exchange_kernel,
        in_specs=[pl.BlockSpec(memory_space=pl.ANY)],
        out_specs=pl.BlockSpec(memory_space=pltpu.VMEM),
        out_shape=jax.ShapeDtypeStruct((4, 4, 4, 4, 16, 128), bf16),
        scratch_shapes=[
            pltpu.VMEM((4, 17, 16, 128), bf16),
            pltpu.VMEM((4, 3, 17, 16, 128), bf16),
            pltpu.VMEM((4, 4, 4, 16, 128), f32),
            pltpu.VMEM((4, 4, 5, 16, 128), bf16),
            pltpu.VMEM((4, 3, 5, 16, 128), bf16),
            pltpu.VMEM((4, 4, 16, 128), f32),
            pltpu.VMEM((4, 4, 2, 16, 128), bf16),
            pltpu.VMEM((4, 3, 2, 16, 128), bf16),
            pltpu.SemaphoreType.DMA((4,)),
            pltpu.SemaphoreType.DMA((6, 4, 3)),
            pltpu.SemaphoreType.DMA((6, 4, 3)),
        ],
        compiler_params=pltpu.CompilerParams(collective_id=1, has_side_effects=True, vmem_limit_bytes=32 * 2**20),
    )(part)


def norm_kernel(sum_ref, out_ref):
    tiles = [sum_ref[0, 0, n].astype(f32) for n in range(32)]
    square = sum(t * t for t in tiles)
    mean = jnp.sum(square, axis=1, keepdims=True) * (1.0 / 4096)
    scale = 1.0 / jnp.sqrt(mean + 1e-06)
    for n in range(32):
        out_ref[0, :, 128 * n:128 * n + 128] = tiles[n] * scale


def norm_call(summed):
    return pl.pallas_call(
        norm_kernel, grid=(2, 4),
        in_specs=[pl.BlockSpec((1, 1, 32, 16, 128), lambda w, p: (p, w, 0, 0, 0))],
        out_specs=pl.BlockSpec((1, 16, 4096), lambda w, p: (w, p, 0)),
        out_shape=jax.ShapeDtypeStruct((2, 64, 4096), f32),
    )(summed.reshape(4, 2, 32, 16, 128))


def on_device(tokens, lengths, feature_table, short_filter, long_filter, queries):
    first = (lax.axis_index("ctx") * 256).astype(jnp.int32).reshape(1)
    hot, tab = prep_call(tokens, feature_table, short_filter)
    mixer_field, part = main_call(first, lengths, hot, tab, long_filter, queries)
    return mixer_field, norm_call(exchange_call(part))


def solution(mesh):
    return jax.shard_map(
        on_device,
        mesh=mesh,
        in_specs=(P("batch", "ctx"), P("batch"), P(), P(), P(), P()),
        out_specs=(P("batch", "ctx", None), P("batch", None, None)),
        check_vma=False,
    )
```

```python
import functools

import jax
import jax.numpy as jnp
from jax import lax
from jax.experimental import pallas as pl
from jax.experimental.pallas import tpu as pltpu
from jax.sharding import PartitionSpec as P

bf16, f32 = jnp.bfloat16, jnp.float32
CODES = (65, 67, 71, 84, 97, 99, 103, 116)
STRIDES = (16, 4, 1)
MESH = pl.DeviceIdType.MESH
CB = 512
WIDE = 1024
GPC = CB // 16
T = 128
LOWEST = -1e38


def prep_kernel(tok_hbm, rows_s, sf_hbm, oh_ref, tab_ref, sf_s, tok_s, prev_s, sf_sem, tok_sem,
                send_sem, recv_sem):
    me = lax.axis_index("ctx")
    core = lax.axis_index("batch")
    nxt, prv = lax.rem(me + 1, 64), lax.rem(me + 63, 64)
    barrier = pltpu.get_barrier_semaphore()
    pl.semaphore_signal(barrier, inc=1, device_id=(core, prv), device_id_type=MESH)
    load_tok = pltpu.make_async_copy(tok_hbm, tok_s, tok_sem)
    load_tok.start()
    load_sf = pltpu.make_async_copy(sf_hbm, sf_s, sf_sem)
    load_sf.start()
    sel_row = lax.broadcasted_iota(jnp.int32, (32, 64), 0)
    sel_col = lax.broadcasted_iota(jnp.int32, (32, 64), 1)
    want = jnp.full((32, 64), -1, jnp.int32)
    for n in range(24):
        want = jnp.where(sel_row == n, CODES[n % 8] - 64, want)
    select = jnp.where(sel_col == want, 1.0, 0.0).astype(bf16)
    e_r = lax.broadcasted_iota(jnp.int32, (T, T), 0)
    e_c = lax.broadcasted_iota(jnp.int32, (T, T), 1)
    eye = jnp.where(e_r == e_c, 1.0, 0.0).astype(bf16)
    load_tok.wait()
    pl.semaphore_wait(barrier, 1)
    send = pltpu.make_async_remote_copy(
        src_ref=tok_s, dst_ref=prev_s, send_sem=send_sem, recv_sem=recv_sem,
        device_id=(core, nxt), device_id_type=MESH)
    send.start()
    load_sf.wait()

    @pl.loop(0, 12288 // WIDE)
    def _(step):
        base = pl.multiple_of(step * WIDE, WIDE)
        cols = pl.ds(base, WIDE)
        picked = jnp.dot(select, rows_s[:, cols], preferred_element_type=f32)[:24]
        gains = jnp.concatenate([jnp.broadcast_to(sf_s[n:n + 1, cols], (8, WIDE)) for n in range(3)], axis=0)
        prod = picked * gains
        hi = prod.astype(bf16).astype(f32)
        rest = prod - hi
        mid = rest.astype(bf16).astype(f32)
        low = rest - mid
        stacked = jnp.concatenate([hi, mid, low, jnp.zeros((56, WIDE), f32)], axis=0).astype(bf16)
        for u in range(WIDE // T):
            turned = lax.dot_general(eye, stacked[:, T * u:T * u + T], (((1,), (1,)), ((), ())),
                                     preferred_element_type=f32)
            tab_ref[pl.ds(base + T * u, T), :] = turned.astype(bf16)

    codes = jnp.zeros((8, 384), jnp.int32)
    code_row = lax.broadcasted_iota(jnp.int32, (8, 384), 0)
    for n in range(8):
        codes = jnp.where(code_row == n, CODES[n], codes)
    send.wait()
    prev = jnp.where(me == 0, -1, prev_s[...])
    for w in range(2):
        ext = jnp.concatenate([prev[w:w + 1], tok_s[w:w + 1]], axis=1)
        hot = [jnp.where(jnp.broadcast_to(ext[:, 128 - k:512 - k], (8, 384)) == codes, 1.0, 0.0) for k in range(3)]
        full = jnp.concatenate(hot * 3 + [jnp.zeros((8, 384), f32)], axis=0).astype(bf16)
        oh_ref[:, 128 * w:128 * w + 128] = full[:, :128]
        oh_ref[:, 256 + 256 * w:512 + 256 * w] = full[:, 128:]


def prep_call(tokens, table, short_filter):
    vmem = pl.BlockSpec(memory_space=pltpu.VMEM)
    hbm = pl.BlockSpec(memory_space=pltpu.HBM)
    return pl.pallas_call(
        prep_kernel,
        in_specs=[hbm, vmem, hbm],
        out_specs=[vmem, vmem],
        out_shape=[jax.ShapeDtypeStruct((80, 768), bf16), jax.ShapeDtypeStruct((12288, 128), bf16)],
        scratch_shapes=[pltpu.VMEM((3, 12288), f32), pltpu.VMEM((2, 256), jnp.int32),
                        pltpu.VMEM((2, 256), jnp.int32)] + [pltpu.SemaphoreType.DMA] * 4,
        compiler_params=pltpu.CompilerParams(collective_id=0, has_side_effects=True, vmem_limit_bytes=32 * 2**20),
    )(tokens, lax.slice(table, (64, 0), (128, 12288)), short_filter)


def main_kernel(oh_ref, tq_ref, tk_ref, tv_ref, h_ref, qry_ref, mix_ref, m_ref, s_ref, g_s):
    i = pl.program_id(0)
    oh = oh_ref[...]
    dot = functools.partial(jnp.dot, preferred_element_type=f32)
    k = dot(tk_ref[...][:, :80], oh)
    v = dot(tv_ref[...][:, :80], oh)
    g_s[...] = (k * v).astype(bf16)
    s_i = lax.broadcasted_iota(jnp.int32, (T, T), 0)
    t_i = lax.broadcasted_iota(jnp.int32, (T, T), 1)
    upper = t_i >= s_i
    h = h_ref[...].astype(f32)
    gate = dot(tq_ref[...][:, :80], oh[:, 256:])
    for j in range(GPC):
        circ = pltpu.roll(jnp.broadcast_to(h[j:j + 1], (T, T)), 0, 1, stride=1, stride_axis=0)
        toep = jnp.concatenate([jnp.where(upper, 0.0, circ), jnp.where(upper, circ, 0.0)], axis=0).astype(bf16)
        rows = pl.ds(16 * j, 16)
        q = gate[16 * j:16 * j + 16]
        blk = [g_s[rows, pl.ds(T * b, T)] for b in range(6)]
        lhs = jnp.concatenate([
            jnp.concatenate([blk[0], blk[2]], axis=1),
            jnp.concatenate([blk[2], blk[3]], axis=1),
            jnp.concatenate([blk[1], blk[4]], axis=1),
            jnp.concatenate([blk[4], blk[5]], axis=1)], axis=0)
        conv = dot(lhs, toep)
        conv = jnp.concatenate([conv[16 * b:16 * b + 16] for b in range(4)], axis=1)
        m_ref[rows, :] = (q * conv).astype(bf16)
    m = m_ref[...]
    sc = dot(qry_ref[...], m)

    @pl.when(i == 0)
    def _():
        s_ref[...] = sc

    @pl.when(i > 0)
    def _():
        s_ref[...] += sc
    for w in range(2):
        mix_ref[w] = m[:, 256 * w:256 * w + 256].T


def main_call(oh, tab, h, qry):
    n = 4096 // CB
    return pl.pallas_call(
        main_kernel, grid=(n,),
        in_specs=[
            pl.BlockSpec((80, 768), lambda i: (0, 0)),
            pl.BlockSpec((CB, 128), lambda i: (i, 0)),
            pl.BlockSpec((CB, 128), lambda i: (i + n, 0)),
            pl.BlockSpec((CB, 128), lambda i: (i + 2 * n, 0)),
            pl.BlockSpec((GPC, 128), lambda i: (i, 0)),
            pl.BlockSpec((64, CB), lambda i: (0, i))],
        out_specs=[pl.BlockSpec((2, 256, CB), lambda i: (0, 0, i)),
                   pl.BlockSpec((CB, 512), lambda i: (i, 0)),
                   pl.BlockSpec((64, 512), lambda i: (0, 0))],
        out_shape=[jax.ShapeDtypeStruct((2, 256, 4096), bf16), jax.ShapeDtypeStruct((4096, 512), bf16),
                   jax.ShapeDtypeStruct((64, 512), f32)],
        scratch_shapes=[pltpu.VMEM((CB, 768), bf16)],
        compiler_params=pltpu.CompilerParams(vmem_limit_bytes=32 * 2**20, dimension_semantics=("arbitrary",)),
    )(oh, tab, tab, tab, h, qry)


def exchange_kernel(len_ref, s_ref, m_ref, out_ref, part_s, r1, s1f, s2, r2, r3, send_sem, recv_sem):
    me = lax.axis_index("ctx")
    core = lax.axis_index("batch")
    coord = [lax.rem(me // st, 4) for st in STRIDES]
    peer = [[me + (lax.rem(coord[a] + d, 4) - coord[a]) * STRIDES[a] for d in range(4)] for a in range(3)]

    def mixed(values, p, stage):
        first, second = values[(p + stage) % 3], values[(p + stage + 1) % 3]
        return first + core * (second - first)

    mine = [[mixed(coord, p, s) for s in range(3)] for p in range(4)]
    peers = [[[mixed([peer[a][d] for a in range(3)], p, s) for d in range(4)] for s in range(3)] for p in range(4)]
    barrier = pltpu.get_barrier_semaphore()
    for a in range(3):
        for d in range(1, 4):
            pl.semaphore_signal(barrier, inc=1, device_id=(core, peer[a][d]), device_id_type=MESH)
    lane = lax.broadcasted_iota(jnp.int32, (16, 128), 1)

    def top_tile(top):
        hi = top.astype(bf16).astype(f32)
        mid = (top - hi).astype(bf16).astype(f32)
        low = top - hi - mid
        return jnp.where(lane == 0, hi, jnp.where(lane == 1, mid, jnp.where(lane == 2, low, 0.0))).astype(bf16)

    position = lax.broadcasted_iota(jnp.int32, (64, 256), 1) + me * 256
    for w in range(2):
        half = slice(256 * w, 256 * w + 256)
        scores = s_ref[:, half] * (4096 ** -0.5)
        valid = position < len_ref[w]
        top = jnp.max(jnp.where(valid, scores, LOWEST), axis=1, keepdims=True)
        shifted = jnp.where(valid, scores - top, 0.0)
        weights = jnp.where(valid, jnp.exp(shifted), 0.0).astype(bf16)
        for c in range(16):
            summed = lax.dot_general(weights, m_ref[256 * c:256 * c + 256, half], (((1,), (1,)), ((), ())),
                                     preferred_element_type=f32).astype(bf16)
            for p in range(4):
                for u in range(2):
                    part_s[2 * w + c // 8, p, 2 * (c % 8) + u] = summed[16 * p:16 * p + 16, T * u:T * u + T]
        for p in range(4):
            tile = top_tile(top[16 * p:16 * p + 16])
            for n in range(2):
                part_s[2 * w + n, p, 16] = tile
    pl.semaphore_wait(barrier, 9)
    sends = []

    def remote(src, dst, phase, p, d, stage):
        return pltpu.make_async_remote_copy(
            src_ref=src, dst_ref=dst, send_sem=send_sem.at[phase, p, d - 1], recv_sem=recv_sem.at[phase, p, d - 1],
            device_id=(core, peers[p][stage][d]), device_id_type=MESH)

    def go(*args):
        copy = remote(*args)
        copy.start()
        sends.append(copy)

    for p in range(4):
        for d in (2, 1, 3):
            go(part_s.at[lax.rem(mine[p][0] + d, 4), p], r1.at[p, d - 1], 0, p, d, 0)

    def read_top(tile):
        return jnp.sum(tile.astype(f32), axis=1, keepdims=True)

    def merged(tops):
        top = functools.reduce(jnp.maximum, tops)
        return top, [jnp.exp(t - top) for t in tops]

    tops1 = []
    for p in range(4):
        own = part_s.at[mine[p][0], p]
        for d in (1, 2, 3):
            remote(own, r1.at[p, d - 1], 0, p, d, 0).wait_recv()
        sources = [own] + [r1.at[p, d] for d in range(3)]
        top, gains = merged([read_top(s[16]) for s in sources])
        tops1.append(top)
        tile = top_tile(top)
        for j in range(4):
            for i in range(4):
                total = sum(g * s[4 * j + i].astype(f32) for g, s in zip(gains, sources))
                s1f[p, j, i] = total
                s2[p, j, i] = total.astype(bf16)
            s2[p, j, 4] = tile
        for d in (2, 1, 3):
            go(s2.at[p, lax.rem(mine[p][1] + d, 4)], r2.at[p, d - 1], 1, p, d, 1)
    for p in range(4):
        for d in (1, 2, 3):
            remote(s2.at[p, 0], r2.at[p, d - 1], 1, p, d, 1).wait_recv()
        top, gains = merged([tops1[p]] + [read_top(r2[p, d, 4]) for d in range(3)])
        here = r3.at[p, mine[p][2]]
        here[4] = top_tile(top)
        for i in range(4):
            total = gains[0] * s1f[p, mine[p][1], i]
            for d in range(3):
                total += gains[d + 1] * r2[p, d, i].astype(f32)
            here[i] = total.astype(bf16)
        for d in (2, 1, 3):
            go(here, here, 2, p, d, 2)
    for p in range(4):
        for d in (1, 2, 3):
            there = r3.at[p, lax.rem(mine[p][2] + 4 - d, 4)]
            remote(there, there, 2, p, d, 2).wait_recv()
        top, gains = merged([read_top(r3[p, k, 4]) for k in range(4)])
        spot = out_ref.at[p, mine[p][0], mine[p][1]]
        for i in range(4):
            total = gains[0] * r3[p, 0, i].astype(f32)
            for k in range(1, 4):
                total += gains[k] * r3[p, k, i].astype(f32)
            spot[i] = total.astype(bf16)
        for d in (2, 1, 3):
            go(spot, spot, 3, p, d, 1)
    for p in range(4):
        for d in (1, 2, 3):
            spot = out_ref.at[p, mine[p][0], lax.rem(mine[p][1] + 4 - d, 4)]
            remote(spot, spot, 3, p, d, 1).wait_recv()
        spot = out_ref.at[p, mine[p][0]]
        for d in (2, 1, 3):
            go(spot, spot, 4, p, d, 0)
    for p in range(4):
        for d in (1, 2, 3):
            spot = out_ref.at[p, lax.rem(mine[p][0] + 4 - d, 4)]
            remote(spot, spot, 4, p, d, 0).wait_recv()
    for copy in sends:
        copy.wait_send()


def exchange_call(lengths, scores, field):
    vmem = pl.BlockSpec(memory_space=pltpu.VMEM)
    return pl.pallas_call(
        exchange_kernel,
        in_specs=[pl.BlockSpec(memory_space=pltpu.SMEM), vmem, vmem],
        out_specs=vmem,
        out_shape=jax.ShapeDtypeStruct((4, 4, 4, 4, 16, 128), bf16),
        scratch_shapes=[
            pltpu.VMEM((4, 4, 17, 16, 128), bf16),
            pltpu.VMEM((4, 3, 17, 16, 128), bf16),
            pltpu.VMEM((4, 4, 4, 16, 128), f32),
            pltpu.VMEM((4, 4, 5, 16, 128), bf16),
            pltpu.VMEM((4, 3, 5, 16, 128), bf16),
            pltpu.VMEM((4, 4, 5, 16, 128), bf16),
            pltpu.SemaphoreType.DMA((5, 4, 3)),
            pltpu.SemaphoreType.DMA((5, 4, 3)),
        ],
        compiler_params=pltpu.CompilerParams(collective_id=1, has_side_effects=True, vmem_limit_bytes=32 * 2**20),
    )(lengths, scores, field)


def norm_kernel(sum_ref, out_ref):
    for p in range(4):
        tiles = [sum_ref[p, 0, n].astype(f32) for n in range(32)]
        square = sum(t * t for t in tiles)
        mean = jnp.sum(square, axis=1, keepdims=True) * (1.0 / 4096)
        scale = 1.0 / jnp.sqrt(mean + 1e-06)
        for n in range(32):
            out_ref[0, 16 * p:16 * p + 16, 128 * n:128 * n + 128] = tiles[n] * scale


def norm_call(summed):
    return pl.pallas_call(
        norm_kernel, grid=(2,),
        in_specs=[pl.BlockSpec((4, 1, 32, 16, 128), lambda w: (0, w, 0, 0, 0))],
        out_specs=pl.BlockSpec((1, 64, 4096), lambda w: (w, 0, 0)),
        out_shape=jax.ShapeDtypeStruct((2, 64, 4096), f32),
        compiler_params=pltpu.CompilerParams(vmem_limit_bytes=16 * 2**20),
    )(summed.reshape(4, 2, 32, 16, 128))


def on_device(tokens, lengths, feature_table, short_filter, long_filter, queries):
    hot, tab = prep_call(tokens, feature_table, short_filter)
    mixer_field, field, scores = main_call(hot, tab, long_filter, queries)
    return mixer_field, norm_call(exchange_call(lengths, scores, field))


def solution(mesh):
    return jax.shard_map(
        on_device,
        mesh=mesh,
        in_specs=(P("batch", "ctx"), P("batch"), P(), P(), P(), P()),
        out_specs=(P("batch", "ctx", None), P("batch", None, None)),
        check_vma=False,
    )
```

```python
import functools

import jax
import jax.numpy as jnp
from jax import lax
from jax.experimental import pallas as pl
from jax.experimental.pallas import tpu as pltpu
from jax.sharding import PartitionSpec as P

bf16, f32 = jnp.bfloat16, jnp.float32
CODES = (65, 67, 71, 84, 97, 99, 103, 116)
STRIDES = (16, 4, 1)
MESH = pl.DeviceIdType.MESH
CB = 1024
STEPS = 4096 // CB
UNIT = 256
WIDE = 1024
T = 128
LOWEST = -1e38
VMEM_LIMIT = 60 * 2**20


def build_tables(rows_s, sf_s, tab_s):
    sel_row = lax.broadcasted_iota(jnp.int32, (32, 64), 0)
    sel_col = lax.broadcasted_iota(jnp.int32, (32, 64), 1)
    want = jnp.full((32, 64), -1, jnp.int32)
    for n in range(24):
        want = jnp.where(sel_row == n, CODES[n % 8] - 64, want)
    select = jnp.where(sel_col == want, 1.0, 0.0).astype(bf16)
    e_r = lax.broadcasted_iota(jnp.int32, (T, T), 0)
    e_c = lax.broadcasted_iota(jnp.int32, (T, T), 1)
    eye = jnp.where(e_r == e_c, 1.0, 0.0).astype(bf16)

    @pl.loop(0, 12288 // WIDE)
    def _(step):
        base = pl.multiple_of(step * WIDE, WIDE)
        cols = pl.ds(base, WIDE)
        picked = jnp.dot(select, rows_s[:, cols], preferred_element_type=f32)[:24]
        gains = jnp.concatenate([jnp.broadcast_to(sf_s[n:n + 1, cols], (8, WIDE)) for n in range(3)], axis=0)
        prod = picked * gains
        hi = prod.astype(bf16).astype(f32)
        rest = prod - hi
        mid = rest.astype(bf16).astype(f32)
        low = rest - mid
        stacked = jnp.concatenate([hi, mid, low, jnp.zeros((56, WIDE), f32)], axis=0).astype(bf16)
        for u in range(WIDE // T):
            turned = lax.dot_general(eye, stacked[:, T * u:T * u + T], (((1,), (1,)), ((), ())),
                                     preferred_element_type=f32)
            tab_s[pl.ds(base + T * u, T), :] = turned.astype(bf16)


def build_hot(prev, tok_s, oh_s):
    codes = jnp.zeros((8, 384), jnp.int32)
    code_row = lax.broadcasted_iota(jnp.int32, (8, 384), 0)
    for n in range(8):
        codes = jnp.where(code_row == n, CODES[n], codes)
    for w in range(2):
        ext = jnp.concatenate([prev[w:w + 1], tok_s[w:w + 1]], axis=1)
        hot = [jnp.where(jnp.broadcast_to(ext[:, 128 - k:512 - k], (8, 384)) == codes, 1.0, 0.0) for k in range(3)]
        full = jnp.concatenate(hot * 3 + [jnp.zeros((8, 384), f32)], axis=0).astype(bf16)
        oh_s[:, 128 * w:128 * w + 128] = full[:, :128]
        oh_s[:, 256 + 256 * w:512 + 256 * w] = full[:, 128:]


def mix_block(step, tab_s, oh_s, h_s, qry_s, g_s, q_s, m_s, s_s, mix_s):
    dot = functools.partial(jnp.dot, preferred_element_type=f32)
    s_i = lax.broadcasted_iota(jnp.int32, (T, T), 0)
    t_i = lax.broadcasted_iota(jnp.int32, (T, T), 1)
    upper = t_i >= s_i
    base = pl.multiple_of(step * CB, CB)
    h = h_s[pl.ds(pl.multiple_of(step * (CB // 16), CB // 16), CB // 16), :].astype(f32)
    for u in range(CB // UNIT):
        rows = pl.ds(UNIT * u, UNIT)
        q, k, v = (dot(tab_s[pl.ds(4096 * n + base + UNIT * u, UNIT), :][:, :80], oh_s[:, 256:] if n == 0 else oh_s[...])
                   for n in range(3))
        g_s[rows, :] = (k * v).astype(bf16)
        q_s[rows, :] = q
    for j in range(CB // 16):
        circ = pltpu.roll(jnp.broadcast_to(h[j:j + 1], (T, T)), 0, 1, stride=1, stride_axis=0)
        toep = jnp.concatenate([jnp.where(upper, 0.0, circ), jnp.where(upper, circ, 0.0)], axis=0).astype(bf16)
        rows = pl.ds(16 * j, 16)
        blk = [g_s[rows, pl.ds(T * b, T)] for b in range(6)]
        lhs = jnp.concatenate([jnp.concatenate([blk[a], blk[b]], axis=1)
                               for a, b in ((0, 2), (2, 3), (1, 4), (4, 5))], axis=0)
        conv = dot(lhs, toep)
        conv = jnp.concatenate([conv[16 * b:16 * b + 16] for b in range(4)], axis=1)
        m_s[pl.ds(base + 16 * j, 16), :] = (q_s[rows, :] * conv).astype(bf16)
    for u in range(CB // UNIT):
        rows = pl.ds(base + UNIT * u, UNIT)
        m = m_s[rows, :]
        for w in range(2):
            mix_s[step, w, :, UNIT * u:UNIT * u + UNIT] = m[:, 256 * w:256 * w + 256].T
    s_s[...] += dot(qry_s[step], m_s[pl.ds(base, CB), :])


def layer_kernel(len_ref, tok_hbm, table_hbm, sf_hbm, h_hbm, qry_hbm, mix_out, sum_out,
                 tok_s, prev_s, rows_s, sf_s, h_s, qry_s, tab_s, oh_s, g_s, q_s, m_ref, s_ref, mix_s,
                 part_s, r1, s1f, s2, r2, r3, out_ref, load_sem, qry_sem, mix_sem, own_sem, tok_sem, send_sem, recv_sem):
    me = lax.axis_index("ctx")
    core = lax.axis_index("batch")
    coord = [lax.rem(me // st, 4) for st in STRIDES]
    peer = [[me + (lax.rem(coord[a] + d, 4) - coord[a]) * STRIDES[a] for d in range(4)] for a in range(3)]

    def mixed(values, p, stage):
        first, second = values[(p + stage) % 3], values[(p + stage + 1) % 3]
        return first + core * (second - first)

    mine = [[mixed(coord, p, s) for s in range(3)] for p in range(4)]
    peers = [[[mixed([peer[a][d] for a in range(3)], p, s) for d in range(4)] for s in range(3)] for p in range(4)]
    barrier = pltpu.get_barrier_semaphore()
    for a in range(3):
        for d in range(1, 4):
            pl.semaphore_signal(barrier, inc=1, device_id=(core, peer[a][d]), device_id_type=MESH)
    nxt, prv = lax.rem(me + 1, 64), lax.rem(me + 63, 64)
    pl.semaphore_signal(barrier, inc=1, device_id=(core, prv), device_id_type=MESH)
    loads = [pltpu.make_async_copy(src, dst, load_sem.at[n]) for n, (src, dst) in enumerate((
        (tok_hbm, tok_s), (sf_hbm, sf_s), (table_hbm.at[pl.ds(64, 64)], rows_s), (h_hbm, h_s)))]
    for n in range(STEPS):
        loads.append(pltpu.make_async_copy(qry_hbm.at[:, pl.ds(CB * n, CB)], qry_s.at[n], qry_sem.at[n]))
    for load in loads:
        load.start()
    s_ref[...] = jnp.zeros_like(s_ref)
    loads[0].wait()
    pl.semaphore_wait(barrier, 10)
    give = pltpu.make_async_remote_copy(
        src_ref=tok_s, dst_ref=prev_s, send_sem=tok_sem.at[0], recv_sem=tok_sem.at[1],
        device_id=(core, nxt), device_id_type=MESH)
    give.start()
    for load in loads[1:]:
        load.wait()
    build_tables(rows_s, sf_s, tab_s)
    give.wait()
    build_hot(jnp.where(me == 0, -1, prev_s[...]), tok_s, oh_s)

    @pl.loop(0, STEPS)
    def _(step):
        mix_block(step, tab_s, oh_s, h_s, qry_s, g_s, q_s, m_ref, s_ref, mix_s)

    writes = []
    for n in range(STEPS):
        write = pltpu.make_async_copy(mix_s.at[n], mix_out.at[:, :, pl.ds(CB * n, CB)], mix_sem.at[n])
        write.start()
        writes.append(write)
    lane = lax.broadcasted_iota(jnp.int32, (16, 128), 1)

    def top_tile(top):
        hi = top.astype(bf16).astype(f32)
        mid = (top - hi).astype(bf16).astype(f32)
        low = top - hi - mid
        return jnp.where(lane == 0, hi, jnp.where(lane == 1, mid, jnp.where(lane == 2, low, 0.0))).astype(bf16)

    position = lax.broadcasted_iota(jnp.int32, (64, 256), 1) + me * 256
    for w in range(2):
        half = slice(256 * w, 256 * w + 256)
        scores = s_ref[:, half] * (4096 ** -0.5)
        valid = position < len_ref[w]
        top = jnp.max(jnp.where(valid, scores, LOWEST), axis=1, keepdims=True)
        shifted = jnp.where(valid, scores - top, 0.0)
        weights = jnp.where(valid, jnp.exp(shifted), 0.0).astype(bf16)
        for c in range(16):
            summed = lax.dot_general(weights, m_ref[256 * c:256 * c + 256, half], (((1,), (1,)), ((), ())),
                                     preferred_element_type=f32).astype(bf16)
            for p in range(4):
                for u in range(2):
                    part_s[2 * w + c // 8, p, 2 * (c % 8) + u] = summed[16 * p:16 * p + 16, T * u:T * u + T]
        for p in range(4):
            tile = top_tile(top[16 * p:16 * p + 16])
            for n in range(2):
                part_s[2 * w + n, p, 16] = tile
    sends = []

    def remote(src, dst, phase, p, d, stage):
        return pltpu.make_async_remote_copy(
            src_ref=src, dst_ref=dst, send_sem=send_sem.at[phase, p, d - 1], recv_sem=recv_sem.at[phase, p, d - 1],
            device_id=(core, peers[p][stage][d]), device_id_type=MESH)

    def go(*args):
        copy = remote(*args)
        copy.start()
        sends.append(copy)

    for p in range(4):
        for d in (2, 1, 3):
            go(part_s.at[lax.rem(mine[p][0] + d, 4), p], r1.at[p, d - 1], 0, p, d, 0)

    def read_top(tile):
        return jnp.sum(tile.astype(f32), axis=1, keepdims=True)

    def merged(tops):
        top = functools.reduce(jnp.maximum, tops)
        return top, [jnp.exp(t - top) for t in tops]

    tops1 = []
    for p in range(4):
        own = part_s.at[mine[p][0], p]
        for d in (1, 2, 3):
            remote(own, r1.at[p, d - 1], 0, p, d, 0).wait_recv()
        sources = [own] + [r1.at[p, d] for d in range(3)]
        top, gains = merged([read_top(s[16]) for s in sources])
        tops1.append(top)
        tile = top_tile(top)
        for j in range(4):
            for i in range(4):
                total = sum(g * s[4 * j + i].astype(f32) for g, s in zip(gains, sources))
                s1f[p, j, i] = total
                s2[p, j, i] = total.astype(bf16)
            s2[p, j, 4] = tile
        for d in (2, 1, 3):
            go(s2.at[p, lax.rem(mine[p][1] + d, 4)], r2.at[p, d - 1], 1, p, d, 1)
    for p in range(4):
        for d in (1, 2, 3):
            remote(s2.at[p, 0], r2.at[p, d - 1], 1, p, d, 1).wait_recv()
        top, gains = merged([tops1[p]] + [read_top(r2[p, d, 4]) for d in range(3)])
        here = r3.at[p, mine[p][2]]
        here[4] = top_tile(top)
        for i in range(4):
            total = gains[0] * s1f[p, mine[p][1], i]
            for d in range(3):
                total += gains[d + 1] * r2[p, d, i].astype(f32)
            here[i] = total.astype(bf16)
        for d in (2, 1, 3):
            go(here, here, 2, p, d, 2)
    for p in range(4):
        for d in (1, 2, 3):
            there = r3.at[p, lax.rem(mine[p][2] + 4 - d, 4)]
            remote(there, there, 2, p, d, 2).wait_recv()
        top, gains = merged([read_top(r3[p, k, 4]) for k in range(4)])
        spot = out_ref.at[p, mine[p][0], mine[p][1]]
        for i in range(4):
            total = gains[0] * r3[p, 0, i].astype(f32)
            for k in range(1, 4):
                total += gains[k] * r3[p, k, i].astype(f32)
            spot[i] = total.astype(bf16)
        for d in (2, 1, 3):
            go(spot, spot, 3, p, d, 1)
    for p in range(4):
        for d in (1, 2, 3):
            spot = out_ref.at[p, mine[p][0], lax.rem(mine[p][1] + 4 - d, 4)]
            remote(spot, spot, 3, p, d, 1).wait_recv()
        spot = out_ref.at[p, mine[p][0]]
        for d in (2, 1, 3):
            go(spot, sum_out.at[p, mine[p][0]], 4, p, d, 0)
        keep = pltpu.make_async_copy(spot, sum_out.at[p, mine[p][0]], own_sem.at[p])
        keep.start()
        writes.append(keep)
    for p in range(4):
        for d in (1, 2, 3):
            spot = sum_out.at[p, lax.rem(mine[p][0] + 4 - d, 4)]
            remote(spot, spot, 4, p, d, 0).wait_recv()
    for copy in sends:
        copy.wait_send()
    for write in writes:
        write.wait()


def layer_call(lengths, tokens, table, short_filter, long_filter, queries):
    hbm = pl.BlockSpec(memory_space=pltpu.HBM)
    return pl.pallas_call(
        layer_kernel,
        in_specs=[pl.BlockSpec(memory_space=pltpu.SMEM)] + [hbm] * 5,
        out_specs=[hbm, hbm],
        out_shape=[jax.ShapeDtypeStruct((2, 256, 4096), bf16), jax.ShapeDtypeStruct((4, 4, 4, 4, 16, 128), bf16)],
        scratch_shapes=[
            pltpu.VMEM((2, 256), jnp.int32),
            pltpu.VMEM((2, 256), jnp.int32),
            pltpu.VMEM((64, 12288), bf16),
            pltpu.VMEM((3, 12288), f32),
            pltpu.VMEM((256, 128), bf16),
            pltpu.VMEM((STEPS, 64, CB), bf16),
            pltpu.VMEM((12288, 128), bf16),
            pltpu.VMEM((80, 768), bf16),
            pltpu.VMEM((CB, 768), bf16),
            pltpu.VMEM((CB, 512), f32),
            pltpu.VMEM((4096, 512), bf16),
            pltpu.VMEM((64, 512), f32),
            pltpu.VMEM((STEPS, 2, 256, CB), bf16),
            pltpu.VMEM((4, 4, 17, 16, 128), bf16),
            pltpu.VMEM((4, 3, 17, 16, 128), bf16),
            pltpu.VMEM((4, 4, 4, 16, 128), f32),
            pltpu.VMEM((4, 4, 5, 16, 128), bf16),
            pltpu.VMEM((4, 3, 5, 16, 128), bf16),
            pltpu.VMEM((4, 4, 5, 16, 128), bf16),
            pltpu.VMEM((4, 4, 4, 4, 16, 128), bf16),
            pltpu.SemaphoreType.DMA((4,)),
            pltpu.SemaphoreType.DMA((STEPS,)),
            pltpu.SemaphoreType.DMA((STEPS,)),
            pltpu.SemaphoreType.DMA((4,)),
            pltpu.SemaphoreType.DMA((2,)),
            pltpu.SemaphoreType.DMA((5, 4, 3)),
            pltpu.SemaphoreType.DMA((5, 4, 3)),
        ],
        compiler_params=pltpu.CompilerParams(collective_id=0, has_side_effects=True, vmem_limit_bytes=VMEM_LIMIT),
    )(lengths, tokens, table, short_filter, long_filter, queries)


def finish_kernel(mix_in, sum_hbm, mix_out, pool_out, mix_s, in_sem, out_sem, sum_s, pool_s, sum_sem, pool_sem):
    moves, copies, reads = [], [], []
    for n in range(8):
        rows = (n // 4, pl.ds(64 * (n % 4), 64))
        read = pltpu.make_async_copy(mix_in.at[rows], mix_s.at[rows], in_sem.at[n])
        reads.append((rows, read))
    for w in range(2):
        for p in range(4):
            load = pltpu.make_async_copy(sum_hbm.at[p, w], sum_s.at[p, w], sum_sem.at[p, w])
            load.start()
            moves.append(load)
    for rows, read in reads:
        read.start()
    for w in range(2):
        for p in range(4):
            moves[4 * w + p].wait()
            tiles = [sum_s[p, w, n].astype(f32) for n in range(32)]
            square = sum(t * t for t in tiles)
            mean = jnp.sum(square, axis=1, keepdims=True) * (1.0 / 4096)
            scale = 1.0 / jnp.sqrt(mean + 1e-06)
            for n in range(32):
                pool_s[w, 16 * p:16 * p + 16, 128 * n:128 * n + 128] = tiles[n] * scale
            rows = (w, pl.ds(16 * p, 16))
            copy = pltpu.make_async_copy(pool_s.at[rows], pool_out.at[rows], pool_sem.at[w, p])
            copy.start()
            copies.append(copy)
            rows, read = reads[4 * w + p]
            read.wait()
            copy = pltpu.make_async_copy(mix_s.at[rows], mix_out.at[rows], out_sem.at[4 * w + p])
            copy.start()
            copies.append(copy)
    for copy in copies:
        copy.wait()


def finish_call(mixed, summed):
    hbm = pl.BlockSpec(memory_space=pltpu.HBM)
    return pl.pallas_call(
        finish_kernel,
        in_specs=[hbm, hbm],
        out_specs=[hbm, hbm],
        out_shape=[jax.ShapeDtypeStruct((2, 256, 4096), bf16), jax.ShapeDtypeStruct((2, 64, 4096), f32)],
        scratch_shapes=[pltpu.VMEM((2, 256, 4096), bf16), pltpu.SemaphoreType.DMA((8,)), pltpu.SemaphoreType.DMA((8,)),
                        pltpu.VMEM((4, 2, 32, 16, 128), bf16), pltpu.VMEM((2, 64, 4096), f32),
                        pltpu.SemaphoreType.DMA((4, 2)), pltpu.SemaphoreType.DMA((2, 4))],
        compiler_params=pltpu.CompilerParams(vmem_limit_bytes=VMEM_LIMIT),
    )(mixed, summed.reshape(4, 2, 32, 16, 128))


def on_device(tokens, lengths, feature_table, short_filter, long_filter, queries):
    mixed, summed = layer_call(lengths, tokens, feature_table, short_filter, long_filter, queries)
    return finish_call(mixed, summed)


def solution(mesh):
    return jax.shard_map(
        on_device,
        mesh=mesh,
        in_specs=(P("batch", "ctx"), P("batch"), P(), P(), P(), P()),
        out_specs=(P("batch", "ctx", None), P("batch", None, None)),
        check_vma=False,
    )
```

```python
import functools

import jax
import jax.numpy as jnp
from jax import lax
from jax.experimental import pallas as pl
from jax.experimental.pallas import tpu as pltpu
from jax.sharding import PartitionSpec as P

bf16, f32 = jnp.bfloat16, jnp.float32
CODES = (65, 67, 71, 84, 97, 99, 103, 116)
STRIDES = (16, 4, 1)
MESH = pl.DeviceIdType.MESH
CB = 1024
STEPS = 4096 // CB
UNIT = 256
WIDE = 1024
T = 128
LOWEST = -1e38
VMEM_LIMIT = 54 * 2**20


def build_tables(rows_s, sf_s, tab_s):
    sel_row = lax.broadcasted_iota(jnp.int32, (32, 64), 0)
    sel_col = lax.broadcasted_iota(jnp.int32, (32, 64), 1)
    want = jnp.full((32, 64), -1, jnp.int32)
    for n in range(24):
        want = jnp.where(sel_row == n, CODES[n % 8] - 64, want)
    select = jnp.where(sel_col == want, 1.0, 0.0).astype(bf16)
    e_r = lax.broadcasted_iota(jnp.int32, (T, T), 0)
    e_c = lax.broadcasted_iota(jnp.int32, (T, T), 1)
    eye = jnp.where(e_r == e_c, 1.0, 0.0).astype(bf16)

    @pl.loop(0, 12288 // WIDE)
    def _(step):
        base = pl.multiple_of(step * WIDE, WIDE)
        cols = pl.ds(base, WIDE)
        picked = jnp.dot(select, rows_s[:, cols], preferred_element_type=f32)[:24]
        gains = jnp.concatenate([jnp.broadcast_to(sf_s[n:n + 1, cols], (8, WIDE)) for n in range(3)], axis=0)
        prod = picked * gains
        hi = prod.astype(bf16).astype(f32)
        rest = prod - hi
        mid = rest.astype(bf16).astype(f32)
        low = rest - mid
        stacked = jnp.concatenate([hi, mid, low, jnp.zeros((56, WIDE), f32)], axis=0).astype(bf16)
        for u in range(0, WIDE, T):
            tab_s[pl.ds(base + u, T), :] = stacked[:, u:u + T].T


def build_hot(prev, tok_s, oh_s):
    codes = jnp.zeros((8, 384), jnp.int32)
    code_row = lax.broadcasted_iota(jnp.int32, (8, 384), 0)
    for n in range(8):
        codes = jnp.where(code_row == n, CODES[n], codes)
    for w in range(2):
        ext = jnp.concatenate([prev[w:w + 1], tok_s[w:w + 1]], axis=1)
        hot = [jnp.where(jnp.broadcast_to(ext[:, 128 - k:512 - k], (8, 384)) == codes, 1.0, 0.0) for k in range(3)]
        full = jnp.concatenate(hot * 3 + [jnp.zeros((8, 384), f32)], axis=0).astype(bf16)
        oh_s[:, 128 * w:128 * w + 128] = full[:, :128]
        oh_s[:, 256 + 256 * w:512 + 256 * w] = full[:, 128:]


def mix_block(step, tab_s, oh_s, h_s, qry_s, g_s, q_s, m_s, s_s, mix_s):
    dot = functools.partial(jnp.dot, preferred_element_type=f32)
    s_i = lax.broadcasted_iota(jnp.int32, (T, T), 0)
    t_i = lax.broadcasted_iota(jnp.int32, (T, T), 1)
    upper = t_i >= s_i
    base = pl.multiple_of(step * CB, CB)
    h = h_s[pl.ds(pl.multiple_of(step * (CB // 16), CB // 16), CB // 16), :].astype(f32)
    for u in range(CB // UNIT):
        rows = pl.ds(UNIT * u, UNIT)
        q, k, v = (dot(tab_s[pl.ds(4096 * n + base + UNIT * u, UNIT), :][:, :80], oh_s[:, 256:] if n == 0 else oh_s[...])
                   for n in range(3))
        g_s[rows, :] = (k * v).astype(bf16)
        q_s[rows, :] = q
    for j in range(CB // 16):
        circ = pltpu.roll(jnp.broadcast_to(h[j:j + 1], (T, T)), 0, 1, stride=1, stride_axis=0)
        toep = jnp.concatenate([jnp.where(upper, 0.0, circ), jnp.where(upper, circ, 0.0)], axis=0).astype(bf16)
        rows = pl.ds(16 * j, 16)
        blk = [g_s[rows, pl.ds(T * b, T)] for b in range(6)]
        lhs = jnp.concatenate([jnp.concatenate([blk[a], blk[b]], axis=1)
                               for a, b in ((0, 2), (2, 3), (1, 4), (4, 5))], axis=0)
        conv = dot(lhs, toep)
        conv = jnp.concatenate([conv[16 * b:16 * b + 16] for b in range(4)], axis=1)
        m_s[pl.ds(base + 16 * j, 16), :] = (q_s[rows, :] * conv).astype(bf16)
    for u in range(CB // UNIT):
        rows = pl.ds(base + UNIT * u, UNIT)
        m = m_s[rows, :]
        for w in range(2):
            mix_s[step, w, :, UNIT * u:UNIT * u + UNIT] = m[:, 256 * w:256 * w + 256].T
    s_s[...] += dot(qry_s[step], m_s[pl.ds(base, CB), :])


def layer_kernel(len_ref, tok_hbm, table_hbm, sf_hbm, h_hbm, qry_hbm, mix_s, out_ref,
                 tok_s, prev_s, rows_s, sf_s, h_s, qry_s, tab_s, oh_s, g_s, q_s, m_ref, s_ref,
                 part_s, r1, s1f, s2, r2, r3, load_sem, qry_sem, tok_sem, send_sem, recv_sem):
    me = lax.axis_index("ctx")
    core = lax.axis_index("batch")
    coord = [lax.rem(me // st, 4) for st in STRIDES]
    peer = [[me + (lax.rem(coord[a] + d, 4) - coord[a]) * STRIDES[a] for d in range(4)] for a in range(3)]

    def mixed(values, p, stage):
        first, second = values[(p + stage) % 3], values[(p + stage + 1) % 3]
        return first + core * (second - first)

    mine = [[mixed(coord, p, s) for s in range(3)] for p in range(4)]
    peers = [[[mixed([peer[a][d] for a in range(3)], p, s) for d in range(4)] for s in range(3)] for p in range(4)]
    barrier = pltpu.get_barrier_semaphore()
    for a in range(3):
        for d in range(1, 4):
            pl.semaphore_signal(barrier, inc=1, device_id=(core, peer[a][d]), device_id_type=MESH)
    nxt, prv = lax.rem(me + 1, 64), lax.rem(me + 63, 64)
    pl.semaphore_signal(barrier, inc=1, device_id=(core, prv), device_id_type=MESH)
    loads = [pltpu.make_async_copy(src, dst, load_sem.at[n]) for n, (src, dst) in enumerate((
        (tok_hbm, tok_s), (sf_hbm, sf_s), (table_hbm.at[pl.ds(64, 64)], rows_s), (h_hbm, h_s)))]
    for n in range(STEPS):
        loads.append(pltpu.make_async_copy(qry_hbm.at[:, pl.ds(CB * n, CB)], qry_s.at[n], qry_sem.at[n]))
    for load in loads:
        load.start()
    s_ref[...] = jnp.zeros_like(s_ref)
    loads[0].wait()
    pl.semaphore_wait(barrier, 10)
    give = pltpu.make_async_remote_copy(
        src_ref=tok_s, dst_ref=prev_s, send_sem=tok_sem.at[0], recv_sem=tok_sem.at[1],
        device_id=(core, nxt), device_id_type=MESH)
    give.start()
    for load in loads[1:]:
        load.wait()
    build_tables(rows_s, sf_s, tab_s)
    give.wait()
    build_hot(jnp.where(me == 0, -1, prev_s[...]), tok_s, oh_s)

    @pl.loop(0, STEPS)
    def _(step):
        mix_block(step, tab_s, oh_s, h_s, qry_s, g_s, q_s, m_ref, s_ref, mix_s)

    lane = lax.broadcasted_iota(jnp.int32, (16, 128), 1)

    def top_tile(top):
        hi = top.astype(bf16).astype(f32)
        mid = (top - hi).astype(bf16).astype(f32)
        low = top - hi - mid
        return jnp.where(lane == 0, hi, jnp.where(lane == 1, mid, jnp.where(lane == 2, low, 0.0))).astype(bf16)

    position = lax.broadcasted_iota(jnp.int32, (64, 256), 1) + me * 256
    for w in range(2):
        half = slice(256 * w, 256 * w + 256)
        scores = s_ref[:, half] * (4096 ** -0.5)
        valid = position < len_ref[w]
        top = jnp.max(jnp.where(valid, scores, LOWEST), axis=1, keepdims=True)
        shifted = jnp.where(valid, scores - top, 0.0)
        weights = jnp.where(valid, jnp.exp(shifted), 0.0).astype(bf16)
        for c in range(16):
            summed = lax.dot_general(weights, m_ref[256 * c:256 * c + 256, half], (((1,), (1,)), ((), ())),
                                     preferred_element_type=f32).astype(bf16)
            for p in range(4):
                for u in range(2):
                    part_s[2 * w + c // 8, p, 2 * (c % 8) + u] = summed[16 * p:16 * p + 16, T * u:T * u + T]
        for p in range(4):
            tile = top_tile(top[16 * p:16 * p + 16])
            for n in range(2):
                part_s[2 * w + n, p, 16] = tile
    sends = []

    def remote(src, dst, phase, p, d, stage):
        return pltpu.make_async_remote_copy(
            src_ref=src, dst_ref=dst, send_sem=send_sem.at[phase, p, d - 1], recv_sem=recv_sem.at[phase, p, d - 1],
            device_id=(core, peers[p][stage][d]), device_id_type=MESH)

    def go(*args):
        copy = remote(*args)
        copy.start()
        sends.append(copy)

    for p in range(4):
        for d in (2, 1, 3):
            go(part_s.at[lax.rem(mine[p][0] + d, 4), p], r1.at[p, d - 1], 0, p, d, 0)

    def read_top(tile):
        return jnp.sum(tile.astype(f32), axis=1, keepdims=True)

    def merged(tops):
        top = functools.reduce(jnp.maximum, tops)
        return top, [jnp.exp(t - top) for t in tops]

    tops1 = []
    for p in range(4):
        own = part_s.at[mine[p][0], p]
        for d in (1, 2, 3):
            remote(own, r1.at[p, d - 1], 0, p, d, 0).wait_recv()
        sources = [own] + [r1.at[p, d] for d in range(3)]
        top, gains = merged([read_top(s[16]) for s in sources])
        tops1.append(top)
        tile = top_tile(top)
        for j in range(4):
            for i in range(4):
                total = sum(g * s[4 * j + i].astype(f32) for g, s in zip(gains, sources))
                s1f[p, j, i] = total
                s2[p, j, i] = total.astype(bf16)
            s2[p, j, 4] = tile
        for d in (2, 1, 3):
            go(s2.at[p, lax.rem(mine[p][1] + d, 4)], r2.at[p, d - 1], 1, p, d, 1)
    for p in range(4):
        for d in (1, 2, 3):
            remote(s2.at[p, 0], r2.at[p, d - 1], 1, p, d, 1).wait_recv()
        top, gains = merged([tops1[p]] + [read_top(r2[p, d, 4]) for d in range(3)])
        here = r3.at[p, mine[p][2]]
        here[4] = top_tile(top)
        for i in range(4):
            total = gains[0] * s1f[p, mine[p][1], i]
            for d in range(3):
                total += gains[d + 1] * r2[p, d, i].astype(f32)
            here[i] = total.astype(bf16)
        for d in (2, 1, 3):
            go(here, here, 2, p, d, 2)
    for p in range(4):
        for d in (1, 2, 3):
            there = r3.at[p, lax.rem(mine[p][2] + 4 - d, 4)]
            remote(there, there, 2, p, d, 2).wait_recv()
        top, gains = merged([read_top(r3[p, k, 4]) for k in range(4)])
        spot = out_ref.at[p, mine[p][0], mine[p][1]]
        for i in range(4):
            total = gains[0] * r3[p, 0, i].astype(f32)
            for k in range(1, 4):
                total += gains[k] * r3[p, k, i].astype(f32)
            spot[i] = total.astype(bf16)
        for d in (2, 1, 3):
            go(spot, spot, 3, p, d, 1)
    for p in range(4):
        for d in (1, 2, 3):
            spot = out_ref.at[p, mine[p][0], lax.rem(mine[p][1] + 4 - d, 4)]
            remote(spot, spot, 3, p, d, 1).wait_recv()
        spot = out_ref.at[p, mine[p][0]]
        for d in (2, 1, 3):
            go(spot, spot, 4, p, d, 0)
    for p in range(4):
        for d in (1, 2, 3):
            spot = out_ref.at[p, lax.rem(mine[p][0] + 4 - d, 4)]
            remote(spot, spot, 4, p, d, 0).wait_recv()
    for copy in sends:
        copy.wait_send()


def layer_call(lengths, tokens, table, short_filter, long_filter, queries):
    hbm = pl.BlockSpec(memory_space=pltpu.HBM)
    vmem = pl.BlockSpec(memory_space=pltpu.VMEM)
    return pl.pallas_call(
        layer_kernel,
        in_specs=[pl.BlockSpec(memory_space=pltpu.SMEM)] + [hbm] * 5,
        out_specs=[vmem, vmem],
        out_shape=[pltpu.VMEM((STEPS, 2, 256, CB), bf16), pltpu.VMEM((4, 4, 4, 4, 16, 128), bf16)],
        scratch_shapes=[
            pltpu.VMEM((2, 256), jnp.int32),
            pltpu.VMEM((2, 256), jnp.int32),
            pltpu.VMEM((64, 12288), bf16),
            pltpu.VMEM((3, 12288), f32),
            pltpu.VMEM((256, 128), bf16),
            pltpu.VMEM((STEPS, 64, CB), bf16),
            pltpu.VMEM((12288, 128), bf16),
            pltpu.VMEM((80, 768), bf16),
            pltpu.VMEM((CB, 768), bf16),
            pltpu.VMEM((CB, 512), f32),
            pltpu.VMEM((4096, 512), bf16),
            pltpu.VMEM((64, 512), f32),
            pltpu.VMEM((4, 4, 17, 16, 128), bf16),
            pltpu.VMEM((4, 3, 17, 16, 128), bf16),
            pltpu.VMEM((4, 4, 4, 16, 128), f32),
            pltpu.VMEM((4, 4, 5, 16, 128), bf16),
            pltpu.VMEM((4, 3, 5, 16, 128), bf16),
            pltpu.VMEM((4, 4, 5, 16, 128), bf16),
            pltpu.SemaphoreType.DMA((4,)),
            pltpu.SemaphoreType.DMA((STEPS,)),
            pltpu.SemaphoreType.DMA((2,)),
            pltpu.SemaphoreType.DMA((5, 4, 3)),
            pltpu.SemaphoreType.DMA((5, 4, 3)),
        ],
        compiler_params=pltpu.CompilerParams(collective_id=0, has_side_effects=True, vmem_limit_bytes=VMEM_LIMIT),
    )(lengths, tokens, table, short_filter, long_filter, queries)


def finish_kernel(mix_s, sum_s, mix_out, pool_out, pool_s, mix_sem, pool_sem):
    copies = []
    for n in range(STEPS):
        copy = pltpu.make_async_copy(mix_s.at[n], mix_out.at[:, :, pl.ds(CB * n, CB)], mix_sem.at[n])
        copy.start()
        copies.append(copy)
    for w in range(2):
        for p in range(4):
            tiles = [sum_s[p, w, n].astype(f32) for n in range(32)]
            square = sum(t * t for t in tiles)
            mean = jnp.sum(square, axis=1, keepdims=True) * (1.0 / 4096)
            scale = 1.0 / jnp.sqrt(mean + 1e-06)
            for n in range(32):
                pool_s[w, 16 * p:16 * p + 16, 128 * n:128 * n + 128] = tiles[n] * scale
            rows = (w, pl.ds(16 * p, 16))
            copy = pltpu.make_async_copy(pool_s.at[rows], pool_out.at[rows], pool_sem.at[w, p])
            copy.start()
            copies.append(copy)
    for copy in copies:
        copy.wait()


def finish_call(mixed, summed):
    hbm = pl.BlockSpec(memory_space=pltpu.HBM)
    vmem = pl.BlockSpec(memory_space=pltpu.VMEM)
    return pl.pallas_call(
        finish_kernel,
        in_specs=[vmem, vmem],
        out_specs=[hbm, hbm],
        out_shape=[jax.ShapeDtypeStruct((2, 256, 4096), bf16), jax.ShapeDtypeStruct((2, 64, 4096), f32)],
        scratch_shapes=[pltpu.VMEM((2, 64, 4096), f32), pltpu.SemaphoreType.DMA((STEPS,)), pltpu.SemaphoreType.DMA((2, 4))],
        compiler_params=pltpu.CompilerParams(vmem_limit_bytes=16 * 2**20),
    )(mixed, summed.reshape(4, 2, 32, 16, 128))


def on_device(tokens, lengths, feature_table, short_filter, long_filter, queries):
    mixed, summed = layer_call(lengths, tokens, feature_table, short_filter, long_filter, queries)
    return finish_call(mixed, summed)


def solution(mesh):
    return jax.shard_map(
        on_device,
        mesh=mesh,
        in_specs=(P("batch", "ctx"), P("batch"), P(), P(), P(), P()),
        out_specs=(P("batch", "ctx", None), P("batch", None, None)),
        check_vma=False,
    )
```

```python
import functools

import jax
import jax.numpy as jnp
from jax import lax
from jax.experimental import pallas as pl
from jax.experimental.pallas import tpu as pltpu
from jax.sharding import PartitionSpec as P

bf16, f32 = jnp.bfloat16, jnp.float32
CODES = (65, 67, 71, 84, 97, 99, 103, 116)
STRIDES = (16, 4, 1)
MESH = pl.DeviceIdType.MESH
CB = 1024
STEPS = 4096 // CB
UNIT = 256
WIDE = 1024
T = 128
LOWEST = -1e38
VMEM_LIMIT = 54 * 2**20


def build_tables(rows_s, sf_s, tab_s):
    sel_row = lax.broadcasted_iota(jnp.int32, (32, 64), 0)
    sel_col = lax.broadcasted_iota(jnp.int32, (32, 64), 1)
    want = jnp.full((32, 64), -1, jnp.int32)
    for n in range(24):
        want = jnp.where(sel_row == n, CODES[n % 8] - 64, want)
    select = jnp.where(sel_col == want, 1.0, 0.0).astype(bf16)
    e_r = lax.broadcasted_iota(jnp.int32, (T, T), 0)
    e_c = lax.broadcasted_iota(jnp.int32, (T, T), 1)
    eye = jnp.where(e_r == e_c, 1.0, 0.0).astype(bf16)

    @pl.loop(0, 12288 // WIDE)
    def _(step):
        base = pl.multiple_of(step * WIDE, WIDE)
        cols = pl.ds(base, WIDE)
        picked = jnp.dot(select, rows_s[:, cols], preferred_element_type=f32)[:24]
        gains = jnp.concatenate([jnp.broadcast_to(sf_s[n:n + 1, cols], (8, WIDE)) for n in range(3)], axis=0)
        prod = picked * gains
        hi = prod.astype(bf16).astype(f32)
        rest = prod - hi
        mid = rest.astype(bf16).astype(f32)
        low = rest - mid
        stacked = jnp.concatenate([hi, mid, low, jnp.zeros((56, WIDE), f32)], axis=0).astype(bf16)
        for u in range(0, WIDE, T):
            tab_s[pl.ds(base + u, T), :] = stacked[:, u:u + T].T


def build_hot(prev, tok_s, oh_s):
    codes = jnp.zeros((8, 384), jnp.int32)
    code_row = lax.broadcasted_iota(jnp.int32, (8, 384), 0)
    for n in range(8):
        codes = jnp.where(code_row == n, CODES[n], codes)
    for w in range(2):
        ext = jnp.concatenate([prev[w:w + 1], tok_s[w:w + 1]], axis=1)
        hot = [jnp.where(jnp.broadcast_to(ext[:, 128 - k:512 - k], (8, 384)) == codes, 1.0, 0.0) for k in range(3)]
        full = jnp.concatenate(hot * 3 + [jnp.zeros((8, 384), f32)], axis=0).astype(bf16)
        oh_s[:, 128 * w:128 * w + 128] = full[:, :128]
        oh_s[:, 256 + 256 * w:512 + 256 * w] = full[:, 128:]


def mix_block(step, tab_s, oh_s, h_s, qry_s, g_s, q_s, m_s, s_s, mix_s):
    dot = functools.partial(jnp.dot, preferred_element_type=f32)
    s_i = lax.broadcasted_iota(jnp.int32, (T, T), 0)
    t_i = lax.broadcasted_iota(jnp.int32, (T, T), 1)
    upper = t_i >= s_i
    base = pl.multiple_of(step * CB, CB)
    h = h_s[pl.ds(pl.multiple_of(step * (CB // 16), CB // 16), CB // 16), :].astype(f32)
    for u in range(CB // UNIT):
        rows = pl.ds(UNIT * u, UNIT)
        q, k, v = (dot(tab_s[pl.ds(4096 * n + base + UNIT * u, UNIT), :][:, :80], oh_s[:, 256:] if n == 0 else oh_s[...])
                   for n in range(3))
        g_s[rows, :] = (k * v).astype(bf16)
        q_s[rows, :] = q
    for j in range(CB // 16):
        circ = pltpu.roll(jnp.broadcast_to(h[j:j + 1], (T, T)), 0, 1, stride=1, stride_axis=0)
        toep = jnp.concatenate([jnp.where(upper, 0.0, circ), jnp.where(upper, circ, 0.0)], axis=0).astype(bf16)
        rows = pl.ds(16 * j, 16)
        blk = [g_s[rows, pl.ds(T * b, T)] for b in range(6)]
        lhs = jnp.concatenate([jnp.concatenate([blk[a], blk[b]], axis=1)
                               for a, b in ((0, 2), (2, 3), (1, 4), (4, 5))], axis=0)
        conv = dot(lhs, toep)
        conv = jnp.concatenate([conv[16 * b:16 * b + 16] for b in range(4)], axis=1)
        m_s[pl.ds(base + 16 * j, 16), :] = (q_s[rows, :] * conv).astype(bf16)
    for u in range(CB // UNIT):
        rows = pl.ds(base + UNIT * u, UNIT)
        m = m_s[rows, :]
        for w in range(2):
            mix_s[step, w, :, UNIT * u:UNIT * u + UNIT] = m[:, 256 * w:256 * w + 256].T
    s_s[...] += dot(qry_s[step], m_s[pl.ds(base, CB), :])


def layer_kernel(len_ref, tok_hbm, table_hbm, sf_hbm, h_hbm, qry_hbm, mix_s, out_ref,
                 tok_s, prev_s, rows_s, sf_s, h_s, qry_s, tab_s, oh_s, g_s, q_s, m_ref, s_ref,
                 part_s, r1, s1f, s2, r2, r3, load_sem, qry_sem, tok_sem, send_sem, recv_sem):
    me = lax.axis_index("ctx")
    core = lax.axis_index("batch")
    coord = [lax.rem(me // st, 4) for st in STRIDES]
    peer = [[me + (lax.rem(coord[a] + d, 4) - coord[a]) * STRIDES[a] for d in range(4)] for a in range(3)]

    def mixed(values, p, stage):
        first, second = values[(p + stage) % 3], values[(p + stage + 2) % 3]
        return first + core * (second - first)

    mine = [[mixed(coord, p, s) for s in range(3)] for p in range(4)]
    peers = [[[mixed([peer[a][d] for a in range(3)], p, s) for d in range(4)] for s in range(3)] for p in range(4)]
    barrier = pltpu.get_barrier_semaphore()
    for a in range(3):
        for d in range(1, 4):
            pl.semaphore_signal(barrier, inc=1, device_id=(core, peer[a][d]), device_id_type=MESH)
    nxt, prv = lax.rem(me + 1, 64), lax.rem(me + 63, 64)
    pl.semaphore_signal(barrier, inc=1, device_id=(core, prv), device_id_type=MESH)
    loads = [pltpu.make_async_copy(src, dst, load_sem.at[n]) for n, (src, dst) in enumerate((
        (tok_hbm, tok_s), (sf_hbm, sf_s), (table_hbm.at[pl.ds(64, 64)], rows_s), (h_hbm, h_s)))]
    for n in range(STEPS):
        loads.append(pltpu.make_async_copy(qry_hbm.at[:, pl.ds(CB * n, CB)], qry_s.at[n], qry_sem.at[n]))
    for load in loads:
        load.start()
    s_ref[...] = jnp.zeros_like(s_ref)
    loads[0].wait()
    pl.semaphore_wait(barrier, 10)
    give = pltpu.make_async_remote_copy(
        src_ref=tok_s, dst_ref=prev_s, send_sem=tok_sem.at[0], recv_sem=tok_sem.at[1],
        device_id=(core, nxt), device_id_type=MESH)
    give.start()
    for load in loads[1:]:
        load.wait()
    build_tables(rows_s, sf_s, tab_s)
    give.wait()
    build_hot(jnp.where(me == 0, -1, prev_s[...]), tok_s, oh_s)

    @pl.loop(0, STEPS)
    def _(step):
        mix_block(step, tab_s, oh_s, h_s, qry_s, g_s, q_s, m_ref, s_ref, mix_s)

    lane = lax.broadcasted_iota(jnp.int32, (16, 128), 1)

    def top_tile(top):
        hi = top.astype(bf16).astype(f32)
        mid = (top - hi).astype(bf16).astype(f32)
        low = top - hi - mid
        return jnp.where(lane == 0, hi, jnp.where(lane == 1, mid, jnp.where(lane == 2, low, 0.0))).astype(bf16)

    position = lax.broadcasted_iota(jnp.int32, (64, 256), 1) + me * 256
    for w in range(2):
        half = slice(256 * w, 256 * w + 256)
        scores = s_ref[:, half] * (4096 ** -0.5)
        valid = position < len_ref[w]
        top = jnp.max(jnp.where(valid, scores, LOWEST), axis=1, keepdims=True)
        shifted = jnp.where(valid, scores - top, 0.0)
        weights = jnp.where(valid, jnp.exp(shifted), 0.0).astype(bf16)
        for c in range(16):
            summed = lax.dot_general(weights, m_ref[256 * c:256 * c + 256, half], (((1,), (1,)), ((), ())),
                                     preferred_element_type=f32).astype(bf16)
            for p in range(4):
                for u in range(2):
                    part_s[2 * w + c // 8, p, 2 * (c % 8) + u] = summed[16 * p:16 * p + 16, T * u:T * u + T]
        for p in range(4):
            tile = top_tile(top[16 * p:16 * p + 16])
            for n in range(2):
                part_s[2 * w + n, p, 16] = tile
    sends = []

    def remote(src, dst, phase, p, d, stage):
        return pltpu.make_async_remote_copy(
            src_ref=src, dst_ref=dst, send_sem=send_sem.at[phase, p, d - 1], recv_sem=recv_sem.at[phase, p, d - 1],
            device_id=(core, peers[p][stage][d]), device_id_type=MESH)

    def go(*args):
        copy = remote(*args)
        copy.start()
        sends.append(copy)

    for p in range(4):
        for d in (2, 1, 3):
            go(part_s.at[lax.rem(mine[p][0] + d, 4), p], r1.at[p, d - 1], 0, p, d, 0)

    def read_top(tile):
        return jnp.sum(tile.astype(f32), axis=1, keepdims=True)

    def merged(tops):
        top = functools.reduce(jnp.maximum, tops)
        return top, [jnp.exp(t - top) for t in tops]

    tops1 = []
    for p in range(4):
        own = part_s.at[mine[p][0], p]
        for d in (1, 2, 3):
            remote(own, r1.at[p, d - 1], 0, p, d, 0).wait_recv()
        sources = [own] + [r1.at[p, d] for d in range(3)]
        top, gains = merged([read_top(s[16]) for s in sources])
        tops1.append(top)
        tile = top_tile(top)
        for j in range(4):
            for i in range(4):
                total = sum(g * s[4 * j + i].astype(f32) for g, s in zip(gains, sources))
                s1f[p, j, i] = total
                s2[p, j, i] = total.astype(bf16)
            s2[p, j, 4] = tile
        for d in (2, 1, 3):
            go(s2.at[p, lax.rem(mine[p][1] + d, 4)], r2.at[p, d - 1], 1, p, d, 1)
    for p in range(4):
        for d in (1, 2, 3):
            remote(s2.at[p, 0], r2.at[p, d - 1], 1, p, d, 1).wait_recv()
        top, gains = merged([tops1[p]] + [read_top(r2[p, d, 4]) for d in range(3)])
        here = r3.at[p, mine[p][2]]
        here[4] = top_tile(top)
        for i in range(4):
            total = gains[0] * s1f[p, mine[p][1], i]
            for d in range(3):
                total += gains[d + 1] * r2[p, d, i].astype(f32)
            here[i] = total.astype(bf16)
        for d in (2, 1, 3):
            go(here, here, 2, p, d, 2)
    for p in range(4):
        for d in (1, 2, 3):
            there = r3.at[p, lax.rem(mine[p][2] + 4 - d, 4)]
            remote(there, there, 2, p, d, 2).wait_recv()
        top, gains = merged([read_top(r3[p, k, 4]) for k in range(4)])
        spot = out_ref.at[p, mine[p][0], mine[p][1]]
        for i in range(4):
            total = gains[0] * r3[p, 0, i].astype(f32)
            for k in range(1, 4):
                total += gains[k] * r3[p, k, i].astype(f32)
            spot[i] = total.astype(bf16)
        for d in (2, 1, 3):
            go(spot, spot, 3, p, d, 1)
    for p in range(4):
        for d in (1, 2, 3):
            spot = out_ref.at[p, mine[p][0], lax.rem(mine[p][1] + 4 - d, 4)]
            remote(spot, spot, 3, p, d, 1).wait_recv()
        spot = out_ref.at[p, mine[p][0]]
        for d in (2, 1, 3):
            go(spot, spot, 4, p, d, 0)
    for p in range(4):
        for d in (1, 2, 3):
            spot = out_ref.at[p, lax.rem(mine[p][0] + 4 - d, 4)]
            remote(spot, spot, 4, p, d, 0).wait_recv()
    for copy in sends:
        copy.wait_send()


def layer_call(lengths, tokens, table, short_filter, long_filter, queries):
    hbm = pl.BlockSpec(memory_space=pltpu.HBM)
    vmem = pl.BlockSpec(memory_space=pltpu.VMEM)
    return pl.pallas_call(
        layer_kernel,
        in_specs=[pl.BlockSpec(memory_space=pltpu.SMEM)] + [hbm] * 5,
        out_specs=[vmem, vmem],
        out_shape=[pltpu.VMEM((STEPS, 2, 256, CB), bf16), pltpu.VMEM((4, 4, 4, 4, 16, 128), bf16)],
        scratch_shapes=[
            pltpu.VMEM((2, 256), jnp.int32),
            pltpu.VMEM((2, 256), jnp.int32),
            pltpu.VMEM((64, 12288), bf16),
            pltpu.VMEM((3, 12288), f32),
            pltpu.VMEM((256, 128), bf16),
            pltpu.VMEM((STEPS, 64, CB), bf16),
            pltpu.VMEM((12288, 128), bf16),
            pltpu.VMEM((80, 768), bf16),
            pltpu.VMEM((CB, 768), bf16),
            pltpu.VMEM((CB, 512), f32),
            pltpu.VMEM((4096, 512), bf16),
            pltpu.VMEM((64, 512), f32),
            pltpu.VMEM((4, 4, 17, 16, 128), bf16),
            pltpu.VMEM((4, 3, 17, 16, 128), bf16),
            pltpu.VMEM((4, 4, 4, 16, 128), f32),
            pltpu.VMEM((4, 4, 5, 16, 128), bf16),
            pltpu.VMEM((4, 3, 5, 16, 128), bf16),
            pltpu.VMEM((4, 4, 5, 16, 128), bf16),
            pltpu.SemaphoreType.DMA((4,)),
            pltpu.SemaphoreType.DMA((STEPS,)),
            pltpu.SemaphoreType.DMA((2,)),
            pltpu.SemaphoreType.DMA((5, 4, 3)),
            pltpu.SemaphoreType.DMA((5, 4, 3)),
        ],
        compiler_params=pltpu.CompilerParams(collective_id=0, has_side_effects=True, vmem_limit_bytes=VMEM_LIMIT),
    )(lengths, tokens, table, short_filter, long_filter, queries)


def finish_kernel(mix_s, sum_s, mix_out, pool_out, pool_s, mix_sem, pool_sem):
    copies = []
    for n in range(STEPS):
        copy = pltpu.make_async_copy(mix_s.at[n], mix_out.at[:, :, pl.ds(CB * n, CB)], mix_sem.at[n])
        copy.start()
        copies.append(copy)
    for w in range(2):
        for p in range(4):
            tiles = [sum_s[p, w, n].astype(f32) for n in range(32)]
            square = sum(t * t for t in tiles)
            mean = jnp.sum(square, axis=1, keepdims=True) * (1.0 / 4096)
            scale = 1.0 / jnp.sqrt(mean + 1e-06)
            for n in range(32):
                pool_s[w, 16 * p:16 * p + 16, 128 * n:128 * n + 128] = tiles[n] * scale
            rows = (w, pl.ds(16 * p, 16))
            copy = pltpu.make_async_copy(pool_s.at[rows], pool_out.at[rows], pool_sem.at[w, p])
            copy.start()
            copies.append(copy)
    for copy in copies:
        copy.wait()


def finish_call(mixed, summed):
    hbm = pl.BlockSpec(memory_space=pltpu.HBM)
    vmem = pl.BlockSpec(memory_space=pltpu.VMEM)
    return pl.pallas_call(
        finish_kernel,
        in_specs=[vmem, vmem],
        out_specs=[hbm, hbm],
        out_shape=[jax.ShapeDtypeStruct((2, 256, 4096), bf16), jax.ShapeDtypeStruct((2, 64, 4096), f32)],
        scratch_shapes=[pltpu.VMEM((2, 64, 4096), f32), pltpu.SemaphoreType.DMA((STEPS,)), pltpu.SemaphoreType.DMA((2, 4))],
        compiler_params=pltpu.CompilerParams(vmem_limit_bytes=16 * 2**20),
    )(mixed, summed.reshape(4, 2, 32, 16, 128))


def on_device(tokens, lengths, feature_table, short_filter, long_filter, queries):
    mixed, summed = layer_call(lengths, tokens, feature_table, short_filter, long_filter, queries)
    return finish_call(mixed, summed)


def solution(mesh):
    return jax.shard_map(
        on_device,
        mesh=mesh,
        in_specs=(P("batch", "ctx"), P("batch"), P(), P(), P(), P()),
        out_specs=(P("batch", "ctx", None), P("batch", None, None)),
        check_vma=False,
    )
```

```python
import functools

import jax
import jax.numpy as jnp
from jax import lax
from jax.experimental import pallas as pl
from jax.experimental.pallas import tpu as pltpu
from jax.sharding import PartitionSpec as P

bf16, f32 = jnp.bfloat16, jnp.float32
CODES = (65, 67, 71, 84, 97, 99, 103, 116)
STRIDES = (16, 4, 1)
MESH = pl.DeviceIdType.MESH
CB = 1024
STEPS = 4096 // CB
UNIT = 256
WIDE = 2048
T = 128
LOWEST = -1e38
VMEM_LIMIT = 54 * 2**20


def build_tables(rows_s, sf_s, tab_s):
    sel_row = lax.broadcasted_iota(jnp.int32, (32, 64), 0)
    sel_col = lax.broadcasted_iota(jnp.int32, (32, 64), 1)
    want = jnp.full((32, 64), -1, jnp.int32)
    for n in range(24):
        want = jnp.where(sel_row == n, CODES[n % 8] - 64, want)
    select = jnp.where(sel_col == want, 1.0, 0.0).astype(bf16)
    e_r = lax.broadcasted_iota(jnp.int32, (T, T), 0)
    e_c = lax.broadcasted_iota(jnp.int32, (T, T), 1)
    eye = jnp.where(e_r == e_c, 1.0, 0.0).astype(bf16)

    @pl.loop(0, 12288 // WIDE)
    def _(step):
        base = pl.multiple_of(step * WIDE, WIDE)
        cols = pl.ds(base, WIDE)
        picked = jnp.dot(select, rows_s[:, cols], preferred_element_type=f32)[:24]
        gains = jnp.concatenate([jnp.broadcast_to(sf_s[n:n + 1, cols], (8, WIDE)) for n in range(3)], axis=0)
        prod = picked * gains
        hi = prod.astype(bf16).astype(f32)
        rest = prod - hi
        mid = rest.astype(bf16).astype(f32)
        low = rest - mid
        stacked = jnp.concatenate([hi, mid, low, jnp.zeros((56, WIDE), f32)], axis=0).astype(bf16)
        for u in range(0, WIDE, T):
            tab_s[pl.ds(base + u, T), :] = stacked[:, u:u + T].T


def build_hot(prev, tok_s, oh_s):
    codes = jnp.zeros((8, 384), jnp.int32)
    code_row = lax.broadcasted_iota(jnp.int32, (8, 384), 0)
    for n in range(8):
        codes = jnp.where(code_row == n, CODES[n], codes)
    for w in range(2):
        ext = jnp.concatenate([prev[w:w + 1], tok_s[w:w + 1]], axis=1)
        hot = [jnp.where(jnp.broadcast_to(ext[:, 128 - k:512 - k], (8, 384)) == codes, 1.0, 0.0) for k in range(3)]
        full = jnp.concatenate(hot * 3 + [jnp.zeros((8, 384), f32)], axis=0).astype(bf16)
        oh_s[:, 128 * w:128 * w + 128] = full[:, :128]
        oh_s[:, 256 + 256 * w:512 + 256 * w] = full[:, 128:]


def mix_block(step, tab_s, oh_s, h_s, qry_s, g_s, q_s, m_s, s_s, mix_s):
    dot = functools.partial(jnp.dot, preferred_element_type=f32)
    s_i = lax.broadcasted_iota(jnp.int32, (T, T), 0)
    t_i = lax.broadcasted_iota(jnp.int32, (T, T), 1)
    upper = t_i >= s_i
    base = pl.multiple_of(step * CB, CB)
    h = h_s[pl.ds(pl.multiple_of(step * (CB // 16), CB // 16), CB // 16), :].astype(f32)
    for u in range(CB // UNIT):
        rows = pl.ds(UNIT * u, UNIT)
        q, k, v = (dot(tab_s[pl.ds(4096 * n + base + UNIT * u, UNIT), :][:, :80], oh_s[:, 256:] if n == 0 else oh_s[...])
                   for n in range(3))
        g_s[rows, :] = (k * v).astype(bf16)
        q_s[rows, :] = q
    for j in range(CB // 16):
        circ = pltpu.roll(jnp.broadcast_to(h[j:j + 1], (T, T)), 0, 1, stride=1, stride_axis=0)
        toep = jnp.concatenate([jnp.where(upper, 0.0, circ), jnp.where(upper, circ, 0.0)], axis=0).astype(bf16)
        rows = pl.ds(16 * j, 16)
        blk = [g_s[rows, pl.ds(T * b, T)] for b in range(6)]
        lhs = jnp.concatenate([jnp.concatenate([blk[a], blk[b]], axis=1)
                               for a, b in ((0, 2), (2, 3), (1, 4), (4, 5))], axis=0)
        conv = dot(lhs, toep)
        conv = jnp.concatenate([conv[16 * b:16 * b + 16] for b in range(4)], axis=1)
        m_s[pl.ds(base + 16 * j, 16), :] = (q_s[rows, :] * conv).astype(bf16)
    for u in range(CB // UNIT):
        rows = pl.ds(base + UNIT * u, UNIT)
        m = m_s[rows, :]
        for w in range(2):
            mix_s[step, w, :, UNIT * u:UNIT * u + UNIT] = m[:, 256 * w:256 * w + 256].T
    s_s[...] += dot(qry_s[step], m_s[pl.ds(base, CB), :])


def layer_kernel(len_ref, tok_hbm, table_hbm, sf_hbm, h_hbm, qry_hbm, mix_s, out_ref,
                 tok_s, prev_s, rows_s, sf_s, h_s, qry_s, tab_s, oh_s, g_s, q_s, m_ref, s_ref,
                 part_s, r1, s1f, s2, r2, r3, load_sem, qry_sem, tok_sem, send_sem, recv_sem):
    me = lax.axis_index("ctx")
    core = lax.axis_index("batch")
    coord = [lax.rem(me // st, 4) for st in STRIDES]
    peer = [[me + (lax.rem(coord[a] + d, 4) - coord[a]) * STRIDES[a] for d in range(4)] for a in range(3)]

    def mixed(values, p, stage):
        first, second = values[(p + stage) % 3], values[(p + stage + 2) % 3]
        return first + core * (second - first)

    mine = [[mixed(coord, p, s) for s in range(3)] for p in range(4)]
    peers = [[[mixed([peer[a][d] for a in range(3)], p, s) for d in range(4)] for s in range(3)] for p in range(4)]
    barrier = pltpu.get_barrier_semaphore()
    for a in range(3):
        for d in range(1, 4):
            pl.semaphore_signal(barrier, inc=1, device_id=(core, peer[a][d]), device_id_type=MESH)
    nxt, prv = lax.rem(me + 1, 64), lax.rem(me + 63, 64)
    pl.semaphore_signal(barrier, inc=1, device_id=(core, prv), device_id_type=MESH)
    loads = [pltpu.make_async_copy(src, dst, load_sem.at[n]) for n, (src, dst) in enumerate((
        (tok_hbm, tok_s), (sf_hbm, sf_s), (table_hbm.at[pl.ds(64, 64)], rows_s), (h_hbm, h_s)))]
    for n in range(STEPS):
        loads.append(pltpu.make_async_copy(qry_hbm.at[:, pl.ds(CB * n, CB)], qry_s.at[n], qry_sem.at[n]))
    for load in loads:
        load.start()
    s_ref[...] = jnp.zeros_like(s_ref)
    loads[0].wait()
    pl.semaphore_wait(barrier, 10)
    give = pltpu.make_async_remote_copy(
        src_ref=tok_s, dst_ref=prev_s, send_sem=tok_sem.at[0], recv_sem=tok_sem.at[1],
        device_id=(core, nxt), device_id_type=MESH)
    give.start()
    for load in loads[1:]:
        load.wait()
    build_tables(rows_s, sf_s, tab_s)
    give.wait()
    build_hot(jnp.where(me == 0, -1, prev_s[...]), tok_s, oh_s)

    @pl.loop(0, STEPS)
    def _(step):
        mix_block(step, tab_s, oh_s, h_s, qry_s, g_s, q_s, m_ref, s_ref, mix_s)

    lane = lax.broadcasted_iota(jnp.int32, (16, 128), 1)

    def top_tile(top):
        hi = top.astype(bf16).astype(f32)
        mid = (top - hi).astype(bf16).astype(f32)
        low = top - hi - mid
        return jnp.where(lane == 0, hi, jnp.where(lane == 1, mid, jnp.where(lane == 2, low, 0.0))).astype(bf16)

    position = lax.broadcasted_iota(jnp.int32, (64, 256), 1) + me * 256
    for w in range(2):
        half = slice(256 * w, 256 * w + 256)
        scores = s_ref[:, half] * (4096 ** -0.5)
        valid = position < len_ref[w]
        top = jnp.max(jnp.where(valid, scores, LOWEST), axis=1, keepdims=True)
        shifted = jnp.where(valid, scores - top, 0.0)
        weights = jnp.where(valid, jnp.exp(shifted), 0.0).astype(bf16)
        for c in range(16):
            summed = lax.dot_general(weights, m_ref[256 * c:256 * c + 256, half], (((1,), (1,)), ((), ())),
                                     preferred_element_type=f32).astype(bf16)
            for p in range(4):
                for u in range(2):
                    part_s[2 * w + c // 8, p, 2 * (c % 8) + u] = summed[16 * p:16 * p + 16, T * u:T * u + T]
        for p in range(4):
            tile = top_tile(top[16 * p:16 * p + 16])
            for n in range(2):
                part_s[2 * w + n, p, 16] = tile
    sends = []

    def remote(src, dst, phase, p, d, stage):
        return pltpu.make_async_remote_copy(
            src_ref=src, dst_ref=dst, send_sem=send_sem.at[phase, p, d - 1], recv_sem=recv_sem.at[phase, p, d - 1],
            device_id=(core, peers[p][stage][d]), device_id_type=MESH)

    def go(*args):
        copy = remote(*args)
        copy.start()
        sends.append(copy)

    for p in range(4):
        for d in (2, 1, 3):
            go(part_s.at[lax.rem(mine[p][0] + d, 4), p], r1.at[p, d - 1], 0, p, d, 0)

    def read_top(tile):
        return jnp.sum(tile.astype(f32), axis=1, keepdims=True)

    def merged(tops):
        top = functools.reduce(jnp.maximum, tops)
        return top, [jnp.exp(t - top) for t in tops]

    tops1 = []
    for p in range(4):
        own = part_s.at[mine[p][0], p]
        for d in (1, 2, 3):
            remote(own, r1.at[p, d - 1], 0, p, d, 0).wait_recv()
        sources = [own] + [r1.at[p, d] for d in range(3)]
        top, gains = merged([read_top(s[16]) for s in sources])
        tops1.append(top)
        tile = top_tile(top)
        for j in range(4):
            for i in range(4):
                total = sum(g * s[4 * j + i].astype(f32) for g, s in zip(gains, sources))
                s1f[p, j, i] = total
                s2[p, j, i] = total.astype(bf16)
            s2[p, j, 4] = tile
        for d in (2, 1, 3):
            go(s2.at[p, lax.rem(mine[p][1] + d, 4)], r2.at[p, d - 1], 1, p, d, 1)
    for p in range(4):
        for d in (1, 2, 3):
            remote(s2.at[p, 0], r2.at[p, d - 1], 1, p, d, 1).wait_recv()
        top, gains = merged([tops1[p]] + [read_top(r2[p, d, 4]) for d in range(3)])
        here = r3.at[p, mine[p][2]]
        here[4] = top_tile(top)
        for i in range(4):
            total = gains[0] * s1f[p, mine[p][1], i]
            for d in range(3):
                total += gains[d + 1] * r2[p, d, i].astype(f32)
            here[i] = total.astype(bf16)
        for d in (2, 1, 3):
            go(here, here, 2, p, d, 2)
    for p in range(4):
        for d in (1, 2, 3):
            there = r3.at[p, lax.rem(mine[p][2] + 4 - d, 4)]
            remote(there, there, 2, p, d, 2).wait_recv()
        top, gains = merged([read_top(r3[p, k, 4]) for k in range(4)])
        spot = out_ref.at[p, mine[p][0], mine[p][1]]
        for i in range(4):
            total = gains[0] * r3[p, 0, i].astype(f32)
            for k in range(1, 4):
                total += gains[k] * r3[p, k, i].astype(f32)
            spot[i] = total.astype(bf16)
        for d in (2, 1, 3):
            go(spot, spot, 3, p, d, 1)
    for p in range(4):
        for d in (1, 2, 3):
            spot = out_ref.at[p, mine[p][0], lax.rem(mine[p][1] + 4 - d, 4)]
            remote(spot, spot, 3, p, d, 1).wait_recv()
        spot = out_ref.at[p, mine[p][0]]
        for d in (2, 1, 3):
            go(spot, spot, 4, p, d, 0)
    for p in range(4):
        for d in (1, 2, 3):
            spot = out_ref.at[p, lax.rem(mine[p][0] + 4 - d, 4)]
            remote(spot, spot, 4, p, d, 0).wait_recv()
    for copy in sends:
        copy.wait_send()


def layer_call(lengths, tokens, table, short_filter, long_filter, queries):
    hbm = pl.BlockSpec(memory_space=pltpu.HBM)
    vmem = pl.BlockSpec(memory_space=pltpu.VMEM)
    return pl.pallas_call(
        layer_kernel,
        in_specs=[pl.BlockSpec(memory_space=pltpu.SMEM)] + [hbm] * 5,
        out_specs=[vmem, vmem],
        out_shape=[pltpu.VMEM((STEPS, 2, 256, CB), bf16), pltpu.VMEM((4, 4, 4, 4, 16, 128), bf16)],
        scratch_shapes=[
            pltpu.VMEM((2, 256), jnp.int32),
            pltpu.VMEM((2, 256), jnp.int32),
            pltpu.VMEM((64, 12288), bf16),
            pltpu.VMEM((3, 12288), f32),
            pltpu.VMEM((256, 128), bf16),
            pltpu.VMEM((STEPS, 64, CB), bf16),
            pltpu.VMEM((12288, 128), bf16),
            pltpu.VMEM((80, 768), bf16),
            pltpu.VMEM((CB, 768), bf16),
            pltpu.VMEM((CB, 512), f32),
            pltpu.VMEM((4096, 512), bf16),
            pltpu.VMEM((64, 512), f32),
            pltpu.VMEM((4, 4, 17, 16, 128), bf16),
            pltpu.VMEM((4, 3, 17, 16, 128), bf16),
            pltpu.VMEM((4, 4, 4, 16, 128), f32),
            pltpu.VMEM((4, 4, 5, 16, 128), bf16),
            pltpu.VMEM((4, 3, 5, 16, 128), bf16),
            pltpu.VMEM((4, 4, 5, 16, 128), bf16),
            pltpu.SemaphoreType.DMA((4,)),
            pltpu.SemaphoreType.DMA((STEPS,)),
            pltpu.SemaphoreType.DMA((2,)),
            pltpu.SemaphoreType.DMA((5, 4, 3)),
            pltpu.SemaphoreType.DMA((5, 4, 3)),
        ],
        compiler_params=pltpu.CompilerParams(collective_id=0, has_side_effects=True, vmem_limit_bytes=VMEM_LIMIT),
    )(lengths, tokens, table, short_filter, long_filter, queries)


def finish_kernel(mix_s, sum_s, mix_out, pool_out, pool_s, mix_sem, pool_sem):
    copies = []
    for n in range(STEPS):
        copy = pltpu.make_async_copy(mix_s.at[n], mix_out.at[:, :, pl.ds(CB * n, CB)], mix_sem.at[n])
        copy.start()
        copies.append(copy)
    for w in range(2):
        for p in range(4):
            tiles = [sum_s[p, w, n].astype(f32) for n in range(32)]
            square = sum(t * t for t in tiles)
            mean = jnp.sum(square, axis=1, keepdims=True) * (1.0 / 4096)
            scale = 1.0 / jnp.sqrt(mean + 1e-06)
            for n in range(32):
                pool_s[w, 16 * p:16 * p + 16, 128 * n:128 * n + 128] = tiles[n] * scale
            rows = (w, pl.ds(16 * p, 16))
            copy = pltpu.make_async_copy(pool_s.at[rows], pool_out.at[rows], pool_sem.at[w, p])
            copy.start()
            copies.append(copy)
    for copy in copies:
        copy.wait()


def finish_call(mixed, summed):
    hbm = pl.BlockSpec(memory_space=pltpu.HBM)
    vmem = pl.BlockSpec(memory_space=pltpu.VMEM)
    return pl.pallas_call(
        finish_kernel,
        in_specs=[vmem, vmem],
        out_specs=[hbm, hbm],
        out_shape=[jax.ShapeDtypeStruct((2, 256, 4096), bf16), jax.ShapeDtypeStruct((2, 64, 4096), f32)],
        scratch_shapes=[pltpu.VMEM((2, 64, 4096), f32), pltpu.SemaphoreType.DMA((STEPS,)), pltpu.SemaphoreType.DMA((2, 4))],
        compiler_params=pltpu.CompilerParams(vmem_limit_bytes=16 * 2**20),
    )(mixed, summed.reshape(4, 2, 32, 16, 128))


def on_device(tokens, lengths, feature_table, short_filter, long_filter, queries):
    mixed, summed = layer_call(lengths, tokens, feature_table, short_filter, long_filter, queries)
    return finish_call(mixed, summed)


def solution(mesh):
    return jax.shard_map(
        on_device,
        mesh=mesh,
        in_specs=(P("batch", "ctx"), P("batch"), P(), P(), P(), P()),
        out_specs=(P("batch", "ctx", None), P("batch", None, None)),
        check_vma=False,
    )
```

```python
import functools

import jax
import jax.numpy as jnp
from jax import lax
from jax.experimental import pallas as pl
from jax.experimental.pallas import tpu as pltpu
from jax.sharding import PartitionSpec as P

bf16, f32 = jnp.bfloat16, jnp.float32
CODES = (65, 67, 71, 84, 97, 99, 103, 116)
STRIDES = (16, 4, 1)
MESH = pl.DeviceIdType.MESH
CB = 1024
STEPS = 4096 // CB
UNIT = 256
WIDE = 2048
T = 128
LOWEST = -1e38
VMEM_LIMIT = 54 * 2**20


def build_tables(rows_s, sf_s, tab_s):
    sel_row = lax.broadcasted_iota(jnp.int32, (32, 64), 0)
    sel_col = lax.broadcasted_iota(jnp.int32, (32, 64), 1)
    want = jnp.full((32, 64), -1, jnp.int32)
    for n in range(24):
        want = jnp.where(sel_row == n, CODES[n % 8] - 64, want)
    select = jnp.where(sel_col == want, 1.0, 0.0).astype(bf16)
    e_r = lax.broadcasted_iota(jnp.int32, (T, T), 0)
    e_c = lax.broadcasted_iota(jnp.int32, (T, T), 1)
    eye = jnp.where(e_r == e_c, 1.0, 0.0).astype(bf16)

    @pl.loop(0, 12288 // WIDE)
    def _(step):
        base = pl.multiple_of(step * WIDE, WIDE)
        cols = pl.ds(base, WIDE)
        picked = jnp.dot(select, rows_s[:, cols], preferred_element_type=f32)[:24]
        gains = jnp.concatenate([jnp.broadcast_to(sf_s[n:n + 1, cols], (8, WIDE)) for n in range(3)], axis=0)
        prod = picked * gains
        hi = prod.astype(bf16).astype(f32)
        rest = prod - hi
        mid = rest.astype(bf16).astype(f32)
        low = rest - mid
        stacked = jnp.concatenate([hi, mid, low, jnp.zeros((56, WIDE), f32)], axis=0).astype(bf16)
        for u in range(0, WIDE, T):
            tab_s[pl.ds(base + u, T), :] = stacked[:, u:u + T].T


def build_hot(prev, tok_s, oh_s):
    codes = jnp.zeros((8, 384), jnp.int32)
    code_row = lax.broadcasted_iota(jnp.int32, (8, 384), 0)
    for n in range(8):
        codes = jnp.where(code_row == n, CODES[n], codes)
    for w in range(2):
        ext = jnp.concatenate([prev[w:w + 1], tok_s[w:w + 1]], axis=1)
        hot = [jnp.where(jnp.broadcast_to(ext[:, 128 - k:512 - k], (8, 384)) == codes, 1.0, 0.0) for k in range(3)]
        full = jnp.concatenate(hot * 3 + [jnp.zeros((8, 384), f32)], axis=0).astype(bf16)
        oh_s[:, 128 * w:128 * w + 128] = full[:, :128]
        oh_s[:, 256 + 256 * w:512 + 256 * w] = full[:, 128:]


def mix_block(step, tab_s, oh_s, h_s, qry_s, g_s, q_s, m_s, s_s):
    dot = functools.partial(jnp.dot, preferred_element_type=f32)
    s_i = lax.broadcasted_iota(jnp.int32, (T, T), 0)
    t_i = lax.broadcasted_iota(jnp.int32, (T, T), 1)
    upper = t_i >= s_i
    base = pl.multiple_of(step * CB, CB)
    h = h_s[pl.ds(pl.multiple_of(step * (CB // 16), CB // 16), CB // 16), :].astype(f32)
    for u in range(CB // UNIT):
        rows = pl.ds(UNIT * u, UNIT)
        q, k, v = (dot(tab_s[pl.ds(4096 * n + base + UNIT * u, UNIT), :][:, :80], oh_s[:, 256:] if n == 0 else oh_s[...])
                   for n in range(3))
        g_s[rows, :] = (k * v).astype(bf16)
        q_s[rows, :] = q
    for j in range(CB // 16):
        circ = pltpu.roll(jnp.broadcast_to(h[j:j + 1], (T, T)), 0, 1, stride=1, stride_axis=0)
        toep = jnp.concatenate([jnp.where(upper, 0.0, circ), jnp.where(upper, circ, 0.0)], axis=0).astype(bf16)
        rows = pl.ds(16 * j, 16)
        blk = [g_s[rows, pl.ds(T * b, T)] for b in range(6)]
        lhs = jnp.concatenate([jnp.concatenate([blk[a], blk[b]], axis=1)
                               for a, b in ((0, 2), (2, 3), (1, 4), (4, 5))], axis=0)
        conv = dot(lhs, toep)
        conv = jnp.concatenate([conv[16 * b:16 * b + 16] for b in range(4)], axis=1)
        m_s[pl.ds(base + 16 * j, 16), :] = (q_s[rows, :] * conv).astype(bf16)
    s_s[...] += dot(qry_s[step], m_s[pl.ds(base, CB), :])


def turn_block(step, m_s, mix_s):
    base = pl.multiple_of(step * CB, CB)
    for u in range(CB // UNIT):
        m = m_s[pl.ds(base + UNIT * u, UNIT), :]
        for w in range(2):
            mix_s[step, w, :, UNIT * u:UNIT * u + UNIT] = m[:, 256 * w:256 * w + 256].T


def layer_kernel(len_ref, tok_hbm, table_hbm, sf_hbm, h_hbm, qry_hbm, mix_s, out_ref,
                 tok_s, prev_s, rows_s, sf_s, h_s, qry_s, tab_s, oh_s, g_s, q_s, m_ref, s_ref,
                 part_s, r1, s1f, s2, r2, r3, load_sem, qry_sem, tok_sem, send_sem, recv_sem):
    me = lax.axis_index("ctx")
    core = lax.axis_index("batch")
    coord = [lax.rem(me // st, 4) for st in STRIDES]
    peer = [[me + (lax.rem(coord[a] + d, 4) - coord[a]) * STRIDES[a] for d in range(4)] for a in range(3)]

    def mixed(values, p, stage):
        first, second = values[(p + stage) % 3], values[(p + stage + 2) % 3]
        return first + core * (second - first)

    mine = [[mixed(coord, p, s) for s in range(3)] for p in range(4)]
    peers = [[[mixed([peer[a][d] for a in range(3)], p, s) for d in range(4)] for s in range(3)] for p in range(4)]
    barrier = pltpu.get_barrier_semaphore()
    for a in range(3):
        for d in range(1, 4):
            pl.semaphore_signal(barrier, inc=1, device_id=(core, peer[a][d]), device_id_type=MESH)
    nxt, prv = lax.rem(me + 1, 64), lax.rem(me + 63, 64)
    pl.semaphore_signal(barrier, inc=1, device_id=(core, prv), device_id_type=MESH)
    loads = [pltpu.make_async_copy(src, dst, load_sem.at[n]) for n, (src, dst) in enumerate((
        (tok_hbm, tok_s), (sf_hbm, sf_s), (table_hbm.at[pl.ds(64, 64)], rows_s), (h_hbm, h_s)))]
    for n in range(STEPS):
        loads.append(pltpu.make_async_copy(qry_hbm.at[:, pl.ds(CB * n, CB)], qry_s.at[n], qry_sem.at[n]))
    for load in loads:
        load.start()
    s_ref[...] = jnp.zeros_like(s_ref)
    loads[0].wait()
    pl.semaphore_wait(barrier, 10)
    give = pltpu.make_async_remote_copy(
        src_ref=tok_s, dst_ref=prev_s, send_sem=tok_sem.at[0], recv_sem=tok_sem.at[1],
        device_id=(core, nxt), device_id_type=MESH)
    give.start()
    for load in loads[1:]:
        load.wait()
    build_tables(rows_s, sf_s, tab_s)
    give.wait()
    build_hot(jnp.where(me == 0, -1, prev_s[...]), tok_s, oh_s)

    @pl.loop(0, STEPS)
    def _(step):
        mix_block(step, tab_s, oh_s, h_s, qry_s, g_s, q_s, m_ref, s_ref)

    lane = lax.broadcasted_iota(jnp.int32, (16, 128), 1)

    def top_tile(top):
        hi = top.astype(bf16).astype(f32)
        mid = (top - hi).astype(bf16).astype(f32)
        low = top - hi - mid
        return jnp.where(lane == 0, hi, jnp.where(lane == 1, mid, jnp.where(lane == 2, low, 0.0))).astype(bf16)

    position = lax.broadcasted_iota(jnp.int32, (64, 256), 1) + me * 256
    for w in range(2):
        half = slice(256 * w, 256 * w + 256)
        scores = s_ref[:, half] * (4096 ** -0.5)
        valid = position < len_ref[w]
        top = jnp.max(jnp.where(valid, scores, LOWEST), axis=1, keepdims=True)
        shifted = jnp.where(valid, scores - top, 0.0)
        weights = jnp.where(valid, jnp.exp(shifted), 0.0).astype(bf16)
        for c in range(16):
            summed = lax.dot_general(weights, m_ref[256 * c:256 * c + 256, half], (((1,), (1,)), ((), ())),
                                     preferred_element_type=f32).astype(bf16)
            for p in range(4):
                for u in range(2):
                    part_s[2 * w + c // 8, p, 2 * (c % 8) + u] = summed[16 * p:16 * p + 16, T * u:T * u + T]
        for p in range(4):
            tile = top_tile(top[16 * p:16 * p + 16])
            for n in range(2):
                part_s[2 * w + n, p, 16] = tile
    sends = []

    def remote(src, dst, phase, p, d, stage):
        return pltpu.make_async_remote_copy(
            src_ref=src, dst_ref=dst, send_sem=send_sem.at[phase, p, d - 1], recv_sem=recv_sem.at[phase, p, d - 1],
            device_id=(core, peers[p][stage][d]), device_id_type=MESH)

    def go(*args):
        copy = remote(*args)
        copy.start()
        sends.append(copy)

    for p in range(4):
        for d in (2, 1, 3):
            go(part_s.at[lax.rem(mine[p][0] + d, 4), p], r1.at[p, d - 1], 0, p, d, 0)

    @pl.loop(0, STEPS)
    def _(step):
        turn_block(step, m_ref, mix_s)

    def read_top(tile):
        return jnp.sum(tile.astype(f32), axis=1, keepdims=True)

    def merged(tops):
        top = functools.reduce(jnp.maximum, tops)
        return top, [jnp.exp(t - top) for t in tops]

    tops1 = []
    for p in range(4):
        own = part_s.at[mine[p][0], p]
        for d in (1, 2, 3):
            remote(own, r1.at[p, d - 1], 0, p, d, 0).wait_recv()
        sources = [own] + [r1.at[p, d] for d in range(3)]
        top, gains = merged([read_top(s[16]) for s in sources])
        tops1.append(top)
        tile = top_tile(top)
        for j in range(4):
            for i in range(4):
                total = sum(g * s[4 * j + i].astype(f32) for g, s in zip(gains, sources))
                s1f[p, j, i] = total
                s2[p, j, i] = total.astype(bf16)
            s2[p, j, 4] = tile
        for d in (2, 1, 3):
            go(s2.at[p, lax.rem(mine[p][1] + d, 4)], r2.at[p, d - 1], 1, p, d, 1)
    for p in range(4):
        for d in (1, 2, 3):
            remote(s2.at[p, 0], r2.at[p, d - 1], 1, p, d, 1).wait_recv()
        top, gains = merged([tops1[p]] + [read_top(r2[p, d, 4]) for d in range(3)])
        here = r3.at[p, mine[p][2]]
        here[4] = top_tile(top)
        for i in range(4):
            total = gains[0] * s1f[p, mine[p][1], i]
            for d in range(3):
                total += gains[d + 1] * r2[p, d, i].astype(f32)
            here[i] = total.astype(bf16)
        for d in (2, 1, 3):
            go(here, here, 2, p, d, 2)
    for p in range(4):
        for d in (1, 2, 3):
            there = r3.at[p, lax.rem(mine[p][2] + 4 - d, 4)]
            remote(there, there, 2, p, d, 2).wait_recv()
        top, gains = merged([read_top(r3[p, k, 4]) for k in range(4)])
        spot = out_ref.at[p, mine[p][0], mine[p][1]]
        for i in range(4):
            total = gains[0] * r3[p, 0, i].astype(f32)
            for k in range(1, 4):
                total += gains[k] * r3[p, k, i].astype(f32)
            spot[i] = total.astype(bf16)
        for d in (2, 1, 3):
            go(spot, spot, 3, p, d, 1)
    for p in range(4):
        for d in (1, 2, 3):
            spot = out_ref.at[p, mine[p][0], lax.rem(mine[p][1] + 4 - d, 4)]
            remote(spot, spot, 3, p, d, 1).wait_recv()
        spot = out_ref.at[p, mine[p][0]]
        for d in (2, 1, 3):
            go(spot, spot, 4, p, d, 0)
    for p in range(4):
        for d in (1, 2, 3):
            spot = out_ref.at[p, lax.rem(mine[p][0] + 4 - d, 4)]
            remote(spot, spot, 4, p, d, 0).wait_recv()
    for copy in sends:
        copy.wait_send()


def layer_call(lengths, tokens, table, short_filter, long_filter, queries):
    hbm = pl.BlockSpec(memory_space=pltpu.HBM)
    vmem = pl.BlockSpec(memory_space=pltpu.VMEM)
    return pl.pallas_call(
        layer_kernel,
        in_specs=[pl.BlockSpec(memory_space=pltpu.SMEM)] + [hbm] * 5,
        out_specs=[vmem, vmem],
        out_shape=[pltpu.VMEM((STEPS, 2, 256, CB), bf16), pltpu.VMEM((4, 4, 4, 4, 16, 128), bf16)],
        scratch_shapes=[
            pltpu.VMEM((2, 256), jnp.int32),
            pltpu.VMEM((2, 256), jnp.int32),
            pltpu.VMEM((64, 12288), bf16),
            pltpu.VMEM((3, 12288), f32),
            pltpu.VMEM((256, 128), bf16),
            pltpu.VMEM((STEPS, 64, CB), bf16),
            pltpu.VMEM((12288, 128), bf16),
            pltpu.VMEM((80, 768), bf16),
            pltpu.VMEM((CB, 768), bf16),
            pltpu.VMEM((CB, 512), f32),
            pltpu.VMEM((4096, 512), bf16),
            pltpu.VMEM((64, 512), f32),
            pltpu.VMEM((4, 4, 17, 16, 128), bf16),
            pltpu.VMEM((4, 3, 17, 16, 128), bf16),
            pltpu.VMEM((4, 4, 4, 16, 128), f32),
            pltpu.VMEM((4, 4, 5, 16, 128), bf16),
            pltpu.VMEM((4, 3, 5, 16, 128), bf16),
            pltpu.VMEM((4, 4, 5, 16, 128), bf16),
            pltpu.SemaphoreType.DMA((4,)),
            pltpu.SemaphoreType.DMA((STEPS,)),
            pltpu.SemaphoreType.DMA((2,)),
            pltpu.SemaphoreType.DMA((5, 4, 3)),
            pltpu.SemaphoreType.DMA((5, 4, 3)),
        ],
        compiler_params=pltpu.CompilerParams(collective_id=0, has_side_effects=True, vmem_limit_bytes=VMEM_LIMIT),
    )(lengths, tokens, table, short_filter, long_filter, queries)


def finish_kernel(mix_s, sum_s, mix_out, pool_out, pool_s, mix_sem, pool_sem):
    copies = []
    for n in range(STEPS):
        copy = pltpu.make_async_copy(mix_s.at[n], mix_out.at[:, :, pl.ds(CB * n, CB)], mix_sem.at[n])
        copy.start()
        copies.append(copy)
    for w in range(2):
        for p in range(4):
            tiles = [sum_s[p, w, n].astype(f32) for n in range(32)]
            square = sum(t * t for t in tiles)
            mean = jnp.sum(square, axis=1, keepdims=True) * (1.0 / 4096)
            scale = 1.0 / jnp.sqrt(mean + 1e-06)
            for n in range(32):
                pool_s[w, 16 * p:16 * p + 16, 128 * n:128 * n + 128] = tiles[n] * scale
            rows = (w, pl.ds(16 * p, 16))
            copy = pltpu.make_async_copy(pool_s.at[rows], pool_out.at[rows], pool_sem.at[w, p])
            copy.start()
            copies.append(copy)
    for copy in copies:
        copy.wait()


def finish_call(mixed, summed):
    hbm = pl.BlockSpec(memory_space=pltpu.HBM)
    vmem = pl.BlockSpec(memory_space=pltpu.VMEM)
    return pl.pallas_call(
        finish_kernel,
        in_specs=[vmem, vmem],
        out_specs=[hbm, hbm],
        out_shape=[jax.ShapeDtypeStruct((2, 256, 4096), bf16), jax.ShapeDtypeStruct((2, 64, 4096), f32)],
        scratch_shapes=[pltpu.VMEM((2, 64, 4096), f32), pltpu.SemaphoreType.DMA((STEPS,)), pltpu.SemaphoreType.DMA((2, 4))],
        compiler_params=pltpu.CompilerParams(vmem_limit_bytes=16 * 2**20),
    )(mixed, summed.reshape(4, 2, 32, 16, 128))


def on_device(tokens, lengths, feature_table, short_filter, long_filter, queries):
    mixed, summed = layer_call(lengths, tokens, feature_table, short_filter, long_filter, queries)
    return finish_call(mixed, summed)


def solution(mesh):
    return jax.shard_map(
        on_device,
        mesh=mesh,
        in_specs=(P("batch", "ctx"), P("batch"), P(), P(), P(), P()),
        out_specs=(P("batch", "ctx", None), P("batch", None, None)),
        check_vma=False,
    )
```
